128 devices in a mesh: space: 16 (over x, y), tm: 8 (over z, core).
Axes of the slice: x: 4, y: 4, z: 4, core: 2. Of those that a mesh axis runs over, the one named last changes fastest.
Arguments:
- fluxes: bfloat16 [32, 1024, 512], P('tm', 'space'), may hold values from -6 to 6
- footprints: bfloat16 [65536, 128, 128], P(('space', 'tm')), may hold values from -0.09375 to 0.09375
- block_coords: int32 [3, 65536], P(None, ('space', 'tm')), may hold values from 0 to 1535, as said below
- block_count: int32 [128], P(('space', 'tm')), may hold values from 128 to 512, as said below
- observed: float32 [196608], P('space'), may hold values from -6 to 6
- obs_weight: float32 [196608], P('space'), may hold values from 0.25 to 4
- time_cov: float32 [32, 32], replicated, as said below
- diffusivity: float32 [1024, 512], P('space'), may hold values from 0.04 to 0.24
Outputs:
- misfit: float32 [196608], P(('space', 'tm'))
- gradient: float32 [32, 1024, 512], P('tm', 'space')
The draws below stay inside these ranges and needn't reach their ends.
Inputs may be any that keep to these rules, and one draw needn't show every extreme that they name: `block_coords`: row 0 lies in 0 to 3, row 1 in 0 to 255, row 2 in 0 to 1535; each row reaches its largest value. Slots at or past a device's live count still hold coordinates in range. `block_count`: some device has all 512 slots live. `time_cov`: Symmetric.
All inputs are finite; a program needn't handle non-finite values.
Results may differ from the reference program's by a relative error of at most 0.0029.
Values may be sent and summed in bfloat16 or wider, within the bound.
No kernel may reach another device: no remote copies, remote signals or barrier semaphores. Data moves between devices by JAX's collectives and lax.ppermute only.
A program may use at most 128 MiB of HBM per device.

```python
import math
import jax
import jax.numpy as jnp
from jax import lax

TR = 64
GW = 512
TIME_DEV = 4
NB_DEV = 512
SWEEPS = 4
TIMES = 32
NROWS = 1024
OBS = 196608
NBLOCKS = 65536
N_SPACE = 16
N_TM = 8
DEVICES = 128


def draw_block_coords(key, part):
    key = jax.random.fold_in(key, 11)
    keys = jax.random.split(key, 4)
    total = NB_DEV * DEVICES
    steps = jax.random.randint(keys[0], (total,), 0, TIME_DEV)
    cells = jax.random.randint(keys[1], (total,), 0, TR * GW // 128)
    blocks = jax.random.randint(keys[2], (total,), 0, OBS // 128)
    places = jax.random.randint(keys[3], (3,), 0, total)
    steps = steps.at[places[0]].set(TIME_DEV - 1)
    cells = cells.at[places[1]].set(TR * GW // 128 - 1)
    blocks = blocks.at[places[2]].set(OBS // 128 - 1)
    return jnp.stack([steps, cells, blocks]).astype(jnp.int32)


def draw_block_count(key, part):
    key = jax.random.fold_in(key, 12)
    keys = jax.random.split(key, 2)
    counts = jax.random.randint(keys[0], (DEVICES,), NB_DEV // 4, NB_DEV + 1)
    place = jax.random.randint(keys[1], (), 0, DEVICES)
    return counts.at[place].set(NB_DEV).astype(jnp.int32)


def draw_time_cov(key, part):
    key = jax.random.fold_in(key, 13)
    keys = jax.random.split(key, 2)
    length = jax.random.uniform(keys[0], (), jnp.float32, 4.0, 10.0)
    steps = jnp.arange(TIMES, dtype=jnp.float32)
    apart = jnp.abs(steps[:, None] - steps[None, :])
    noise = jax.random.uniform(keys[1], (TIMES, TIMES), jnp.float32)
    paired = 0.5 * (noise + noise.T)
    return (jnp.exp(-apart / length) * (0.7 + 0.6 * paired)).astype(jnp.float32)


def block_scale(own_key, dims, cuts, low, top_value):
    def one(dim, blocks):
        steps = jax.random.uniform(jax.random.fold_in(jax.random.fold_in(own_key, 6), dim), (blocks,), jnp.float32, low / len(cuts), top_value / len(cuts))
        return jnp.repeat(jnp.exp(steps), dims[dim] // blocks).reshape((-1,) + (1,) * (len(dims) - dim - 1))

    factor_of = one(*cuts[0])
    for cut in cuts[1:]:
        factor_of = factor_of * one(*cut)
    return factor_of


def centred(rng, extent, width, reach, cuts=(), kind=jnp.bfloat16):
    entries = jax.random.normal(rng, extent, jnp.float32) * width
    if len(cuts) > 0:
        entries = block_scale(rng, extent, cuts, -0.22, 0.18) * entries
    return jnp.clip(entries, min=-reach, max=reach).astype(kind)


def setup_inputs(seed: int = 0) -> dict:
    key_of = jax.random.split(jax.random.key(seed), 9)
    return {
        "fluxes": centred(key_of[0], (TIMES, NROWS, GW), 1.0, 6.0, ((0, 8), (1, 16))),
        "footprints": centred(key_of[1], (NBLOCKS, 128, 128), 4096 ** -0.5, 0.09375, ((0, 128),)),
        "block_coords": draw_block_coords(jax.random.fold_in(key_of[8], 71), 0),
        "block_count": draw_block_count(jax.random.fold_in(key_of[8], 71), 0),
        "observed": centred(key_of[4], (OBS,), 1.0, 6.0, ((0, 16),), jnp.float32),
        "obs_weight": jnp.clip(jnp.exp(math.log(4.0) - 2.7725887 * jax.random.uniform(key_of[5], (OBS,), jnp.float32) ** block_scale(key_of[5], (OBS,), ((0, 16),), -0.2, 0.2)), 0.25, 4.0),
        "time_cov": draw_time_cov(jax.random.fold_in(key_of[8], 71), 0),
        "diffusivity": jnp.clip(jnp.exp(math.log(0.24) - 1.7917595 * jax.random.uniform(key_of[7], (NROWS, GW), jnp.float32) ** block_scale(key_of[7], (NROWS, GW), ((0, 16),), -0.2, 0.2)), 0.04, 0.24),
    }


def smooth(field, diffusivity):
    for repeat in range(SWEEPS):
        padded = jnp.pad(field, ((0, 0), (1, 1), (1, 1)))
        laplace = padded[:, 2:, 1:-1] + padded[:, :-2, 1:-1] + padded[:, 1:-1, 2:] + padded[:, 1:-1, :-2] - 4.0 * field
        field = field + diffusivity * laplace
    return field


def reference(fluxes, footprints, block_coords, block_count, observed, obs_weight, time_cov, diffusivity):
    cell_blocks = TR * GW // 128
    all_blocks = N_SPACE * cell_blocks
    flux_rows = fluxes.reshape(TIMES * all_blocks, 128)
    foot_dev = footprints.reshape(DEVICES, NB_DEV, 128, 128)
    coord_dev = jnp.transpose(block_coords.reshape(3, DEVICES, NB_DEV), (1, 0, 2))
    device_ids = jnp.arange(DEVICES, dtype=jnp.int32)
    slot_ids = jnp.arange(NB_DEV, dtype=jnp.int32)

    def locate(coords, count, device):
        space_index = device // N_TM
        time_index = device % N_TM
        target = (time_index * TIME_DEV + coords[0]) * all_blocks + space_index * cell_blocks + coords[1]
        slot_live = (slot_ids < count).astype(jnp.float32)
        return target.astype(jnp.int32), slot_live

    def forward(running, inputs):
        blocks, coords, count, device = inputs
        target, slot_live = locate(coords, count, device)
        pieces = flux_rows[target].astype(jnp.float32)
        contrib = jnp.einsum("boc,bc->bo", blocks.astype(jnp.float32), pieces) * slot_live[:, None]
        return running.at[coords[2]].add(contrib), device

    modelled_blocks = lax.scan(forward, jnp.zeros((OBS // 128, 128), jnp.float32), (foot_dev, coord_dev, block_count, device_ids))[0]
    misfit = obs_weight * (modelled_blocks.reshape(OBS) - observed)
    misfit_half = lax.optimization_barrier(misfit.astype(jnp.bfloat16))
    misfit_rows = misfit_half.reshape(OBS // 128, 128).astype(jnp.float32)

    def backward(running, inputs):
        blocks, coords, count, device = inputs
        target, slot_live = locate(coords, count, device)
        chosen = misfit_rows[coords[2]]
        adjoint = jnp.einsum("boc,bo->bc", blocks.astype(jnp.float32), chosen) * slot_live[:, None]
        return running.at[target].add(adjoint), device

    adjoint_rows = lax.scan(backward, jnp.zeros((TIMES * all_blocks, 128), jnp.float32), (foot_dev, coord_dev, block_count, device_ids))[0]
    grid = adjoint_rows.reshape(TIMES, TR * N_SPACE, GW)
    mixed = jnp.einsum("ts,snc->tnc", time_cov, grid, precision=lax.Precision.HIGHEST)
    gradient = smooth(mixed, diffusivity)
    return misfit, gradient
```

```python
import jax
import jax.numpy as jnp
from jax import lax
from jax.experimental import pallas as pl
from jax.experimental.pallas import tpu as pltpu
from jax.sharding import PartitionSpec as P

SWEEPS = 4
LANES = 128
CHUNKS = 8
EDGE = 8
VMEM = 60 * 1024 * 1024

f32 = jnp.float32
bf16 = jnp.bfloat16


def split3(x):
    hi = x.astype(bf16)
    rest = x - hi.astype(f32)
    mid = rest.astype(bf16)
    low = (rest - mid.astype(f32)).astype(bf16)
    return hi, mid, low


def iota(shape, dim):
    return lax.broadcasted_iota(jnp.int32, shape, dim)


def onehot(equal):
    return jnp.where(equal, 1.0, 0.0).astype(bf16)


def dot(a, b, precision=None):
    return lax.dot_general(
        a, b, (((1,), (0,)), ((), ())), preferred_element_type=f32, precision=precision
    )


def column(row):
    wide = jnp.broadcast_to(row.astype(f32), (LANES, LANES))
    return jnp.transpose(wide, (1, 0)).astype(jnp.int32)


def forward_kernel(count_ref, coords_ref, flux_ref, foot_ref, out_ref, keep_ref, rhs, spread, sems):
    slots = foot_ref.shape[0]
    groups = slots // LANES
    per = slots // CHUNKS
    time_dev, tile_rows, width = flux_ref.shape
    across = width // LANES
    steps = time_dev * tile_rows

    def fetch(k):
        part = pl.ds(k * per, per)
        return pltpu.make_async_copy(foot_ref.at[part], keep_ref.at[part], sems.at[k])

    for k in range(CHUNKS):
        fetch(k).start()

    flux = flux_ref[...].reshape(steps, width)
    flux = jnp.concatenate([flux[:, l * LANES : (l + 1) * LANES] for l in range(across)], axis=0)
    lane = iota((LANES, LANES), 1)
    for g in range(groups):
        cut = slice(g * LANES, (g + 1) * LANES)
        cell = coords_ref[1:2, cut]
        code = (cell % across) * steps + coords_ref[0:1, cut] * tile_rows + cell // across
        code = column(code)
        pick = jnp.concatenate(
            [onehot(code == lane + j * LANES) for j in range(across * steps // LANES)], axis=1
        )
        piece = jnp.transpose(dot(pick, flux), (1, 0))
        even = (lane & 1) == 0
        rhs[g, :LANES, :] = jnp.where(even, piece, 0.0).astype(bf16)
        rhs[g, LANES:, :] = jnp.where(even, 0.0, piece).astype(bf16)

    pair_of_lane = lane // 2
    chunks_per_group = CHUNKS // groups
    for g in range(groups):
        total = jnp.zeros((LANES, LANES), f32)
        for part in range(chunks_per_group):
            fetch(g * chunks_per_group + part).wait()

            def step(i, total, part=part, g=g):
                for j in range(4):
                    p = part * (per // 2) + i * 4 + j
                    b = g * LANES + 2 * p
                    both = jnp.concatenate([keep_ref[b], keep_ref[b + 1]], axis=1)
                    total = jnp.where(pair_of_lane == p, dot(both, rhs[g]), total)
                return total

            total = lax.fori_loop(0, per // 8, step, total)
        parts = split3(jnp.transpose(total, (1, 0)))
        for n in range(3):
            spread[g * LANES : (g + 1) * LANES, n * LANES : (n + 1) * LANES] = parts[n]

    slot = iota((1, slots), 1)
    block = jnp.where(slot < count_ref[0], coords_ref[2:3, :], -1)
    rows = out_ref.shape[0] * out_ref.shape[1]
    cols = out_ref.shape[2] // LANES
    for l in range(cols):
        mine = iota((rows, slots), 0) * cols + l
        full = dot(onehot(mine == block), spread[...])
        summed = full[:, :LANES] + full[:, LANES : 2 * LANES] + full[:, 2 * LANES :]
        out_ref[:, :, l * LANES : (l + 1) * LANES] = summed.reshape(
            out_ref.shape[0], out_ref.shape[1], LANES
        )


def forward(count, coords, fluxes, footprints, devices, obs_blocks):
    per = obs_blocks // devices
    slots = footprints.shape[0]
    vmem = pl.BlockSpec(memory_space=pltpu.VMEM)
    return pl.pallas_call(
        forward_kernel,
        out_shape=(
            jax.ShapeDtypeStruct((devices, 4, per * LANES // 4), f32),
            jax.ShapeDtypeStruct(footprints.shape, bf16),
        ),
        in_specs=[pl.BlockSpec(memory_space=pltpu.SMEM), vmem, vmem, pl.BlockSpec(memory_space=pl.ANY)],
        out_specs=(vmem, vmem),
        scratch_shapes=[
            pltpu.VMEM((slots // LANES, 2 * LANES, LANES), bf16),
            pltpu.VMEM((slots, 3 * LANES), bf16),
            pltpu.SemaphoreType.DMA((CHUNKS,)),
        ],
        compiler_params=pltpu.CompilerParams(vmem_limit_bytes=VMEM),
        name="forward",
    )(count, coords, fluxes, footprints)


def misfit_kernel(sums_ref, weight_ref, observed_ref, out_ref, half_ref):
    total = jnp.sum(sums_ref[...], axis=0)
    misfit = weight_ref[...] * (total - observed_ref[...])
    out_ref[...] = misfit
    half_ref[...] = jnp.broadcast_to(misfit[None], half_ref.shape).astype(bf16)


def misfit_of(sums, weight, observed):
    devices = sums.shape[0]
    shape = sums.shape[1:]
    return pl.pallas_call(
        misfit_kernel,
        out_shape=(
            jax.ShapeDtypeStruct(shape, f32),
            jax.ShapeDtypeStruct((devices,) + shape, bf16),
        ),
        name="misfit",
    )(sums, weight.reshape(shape), observed.reshape(shape))


def adjoint_kernel(
    count_ref,
    coords_ref,
    misfit_ref,
    foot_ref,
    before_ref,
    diff_ref,
    after_ref,
    out_ref,
    contrib,
    spread,
    field,
    other,
    rows_ref,
):
    slots = foot_ref.shape[0]
    groups = slots // LANES
    devices, quarter, wide = misfit_ref.shape
    cols = wide // LANES
    rows = devices * quarter
    lane = iota((LANES, LANES), 1)
    rows_ref[...] = misfit_ref[...].astype(f32).reshape(rows, wide).astype(bf16)
    for g in range(groups):
        block = column(coords_ref[2:3, g * LANES : (g + 1) * LANES])
        chosen = jnp.zeros((LANES, LANES), f32)
        for l in range(cols):
            pick = jnp.concatenate(
                [onehot(block == (lane + j * LANES) * cols + l) for j in range(rows // LANES)], axis=1
            )
            chosen = chosen + dot(pick, rows_ref[:, l * LANES : (l + 1) * LANES])
        contrib[g * LANES : (g + 1) * LANES, :] = chosen

    batch = 16
    sub = iota((batch, LANES), 0)

    def step(i, carry):
        for half in range(2):
            at = pl.multiple_of(i * 2 * batch + half * batch, batch)
            some = contrib[pl.ds(at, batch), :]
            left = jnp.concatenate(
                [jnp.where(sub == j, some, 0.0).astype(bf16) for j in range(batch)], axis=1
            )
            blocks = foot_ref[pl.ds(at, batch)].reshape(batch * LANES, LANES)
            for n, part in enumerate(split3(dot(left, blocks))):
                spread[pl.ds(at, batch), n * LANES : (n + 1) * LANES] = part
        return carry

    lax.fori_loop(0, slots // (2 * batch), step, 0)

    time_dev, ext_rows, width = field.shape
    across = width // LANES
    tile_rows = diff_ref.shape[0]
    steps = time_dev * tile_rows
    slot = iota((1, slots), 1)
    cell = coords_ref[1:2, :]
    code = coords_ref[0:1, :] * tile_rows + cell // across
    code = jnp.where(slot < count_ref[0], code, -1)
    up, inner, down = slice(EDGE - 1, ext_rows - EDGE - 1), slice(EDGE, ext_rows - EDGE), slice(EDGE + 1, ext_rows - EDGE + 1)
    for buffer in (field, other):
        for t in range(time_dev):
            buffer[t, : 2 * EDGE, :] = jnp.zeros((2 * EDGE, width), f32)
            buffer[t, ext_rows - 2 * EDGE :, :] = jnp.zeros((2 * EDGE, width), f32)
    for l in range(across):
        pick = onehot(iota((steps, slots), 0) == jnp.where(cell % across == l, code, -1))
        full = dot(pick, spread[...])
        summed = full[:, :LANES] + full[:, LANES : 2 * LANES] + full[:, 2 * LANES :]
        for t in range(time_dev):
            field[t, 2 * EDGE : 2 * EDGE + tile_rows, l * LANES : (l + 1) * LANES] = summed[
                t * tile_rows : (t + 1) * tile_rows
            ]
    diff = jnp.concatenate([before_ref[...], diff_ref[...], after_ref[...]], axis=0)
    column_of = iota(diff.shape, 1)
    source, target = field, other
    for sweep in range(SWEEPS):
        for t in range(time_dev):
            here = source[t, inner, :]
            left = jnp.where(column_of == 0, 0.0, pltpu.roll(here, 1, 1))
            right = jnp.where(column_of == width - 1, 0.0, pltpu.roll(here, width - 1, 1))
            laplace = source[t, down, :] + source[t, up, :] + right + left - 4.0 * here
            target[t, inner, :] = here + diff * laplace
        source, target = target, source
    half = tile_rows // 2
    first = 2 * EDGE
    for h in range(2):
        edge = first - SWEEPS if h == 0 else first + tile_rows
        for l in range(across):
            cut = slice(l * LANES, (l + 1) * LANES)
            rows_out = [
                source[t, first + h * half : first + (h + 1) * half, cut] for t in range(time_dev)
            ] + [source[t, edge : edge + SWEEPS, cut] for t in range(time_dev)]
            out_ref[h * across + l] = jnp.concatenate(rows_out, axis=0).astype(out_ref.dtype)


def adjoint_of(count, coords, misfit_rows, footprints, before, diffusivity, after, time_dev):
    slots = footprints.shape[0]
    tile_rows, width = diffusivity.shape
    devices, quarter, wide = misfit_rows.shape
    parts = 2 * width // LANES
    vmem = pl.BlockSpec(memory_space=pltpu.VMEM)
    field = pltpu.VMEM((time_dev, tile_rows + 4 * EDGE, width), f32)
    return pl.pallas_call(
        adjoint_kernel,
        out_shape=jax.ShapeDtypeStruct((parts, time_dev * (tile_rows // 2 + SWEEPS), LANES), bf16),
        in_specs=[pl.BlockSpec(memory_space=pltpu.SMEM)] + [vmem] * 6,
        out_specs=vmem,
        scratch_shapes=[
            pltpu.VMEM((slots, LANES), f32),
            pltpu.VMEM((slots, 3 * LANES), bf16),
            field,
            field,
            pltpu.VMEM((devices * quarter, wide), bf16),
        ],
        compiler_params=pltpu.CompilerParams(vmem_limit_bytes=VMEM),
        name="adjoint",
    )(count, coords, misfit_rows, footprints, before, diffusivity, after)


def expanded(cov, rows, per_row, cols, per_col, shift):
    times = cov.shape[0]
    tall = onehot(iota((rows, times), 0) // per_row == iota((rows, times), 1)).astype(f32)
    broad = onehot(iota((times, cols), 1) // per_col == iota((times, cols), 0)).astype(f32)
    full = dot(dot(tall, cov, lax.Precision.HIGHEST), broad, lax.Precision.HIGHEST)
    same = iota((rows, cols), 0) % per_row == iota((rows, cols), 1) % per_col + shift
    return jnp.where(same, full, 0.0)


def spill_kernel(half_ref, cov_ref, parts_ref, out_ref):
    senders, rows, _ = parts_ref.shape
    times = cov_ref.shape[0]
    time_dev = times // senders
    main = rows - time_dev * SWEEPS
    edges = jnp.concatenate(
        [parts_ref[n, main:, :].astype(f32) for n in range(senders)], axis=0
    ).astype(bf16)
    shift = jnp.where(half_ref[0] == 0, SWEEPS, 0)
    wide = expanded(cov_ref[...], times * EDGE, EDGE, times * SWEEPS, SWEEPS, shift)
    out_ref[...] = sum(dot(part, edges) for part in split3(wide))


def mix_spill(half, cov, parts):
    vmem = pl.BlockSpec(memory_space=pltpu.VMEM)
    return pl.pallas_call(
        spill_kernel,
        out_shape=jax.ShapeDtypeStruct((cov.shape[0] * EDGE, LANES), f32),
        in_specs=[pl.BlockSpec(memory_space=pltpu.SMEM), vmem, vmem],
        out_specs=vmem,
        name="mix_spill",
    )(half, cov, parts)


def mix_kernel(half_ref, cov_ref, parts_ref, spill_ref, out_ref):
    senders, rows, _ = parts_ref.shape
    times = cov_ref.shape[0]
    time_dev = times // senders
    tall = (rows - time_dev * SWEEPS) // time_dev
    wide = split3(expanded(cov_ref[...], times * EDGE, EDGE, times * EDGE, EDGE, 0))
    strips = []
    for r in range(tall // EDGE):
        strips.append(
            jnp.concatenate(
                [
                    parts_ref[n, u * tall + r * EDGE : u * tall + (r + 1) * EDGE, :].astype(f32)
                    for n in range(senders)
                    for u in range(time_dev)
                ],
                axis=0,
            ).astype(bf16)
        )
    field = jnp.concatenate(strips, axis=1)
    mixed = dot(wide[0], field) + dot(wide[1], field) + dot(wide[2], field)
    strips = [mixed[:, r * LANES : (r + 1) * LANES] for r in range(tall // EDGE)]
    strips[0] = strips[0] + jnp.where(half_ref[0] == 0, spill_ref[...], 0.0)
    strips[-1] = strips[-1] + jnp.where(half_ref[0] == 0, 0.0, spill_ref[...])
    for t in range(times):
        cut = slice(t * EDGE, (t + 1) * EDGE)
        at = (t % time_dev) * tall
        out_ref[t // time_dev, at : at + tall, :] = jnp.concatenate(
            [strip[cut] for strip in strips], axis=0
        ).astype(out_ref.dtype)


def mix(half, cov, parts, spill):
    senders, rows, _ = parts.shape
    time_dev = cov.shape[0] // senders
    vmem = pl.BlockSpec(memory_space=pltpu.VMEM)
    return pl.pallas_call(
        mix_kernel,
        out_shape=jax.ShapeDtypeStruct((senders, rows - time_dev * SWEEPS, LANES), bf16),
        in_specs=[pl.BlockSpec(memory_space=pltpu.SMEM), vmem, vmem, vmem],
        out_specs=vmem,
        name="mix",
    )(half, cov, parts, spill)


def place_kernel(parts_ref, out_ref):
    time_dev, tile_rows, width = out_ref.shape
    across = width // LANES
    half = tile_rows // 2
    for h in range(2):
        for l in range(across):
            for t in range(time_dev):
                out_ref[t, h * half : (h + 1) * half, l * LANES : (l + 1) * LANES] = parts_ref[
                    h * across + l, t * half : (t + 1) * half, :
                ].astype(f32)


def body(
    fluxes, footprints, block_coords, block_count, observed, obs_weight, time_cov, diffusivity
):
    time_dev, tile_rows, width = fluxes.shape
    n_space, n_tm = lax.axis_size("space"), lax.axis_size("tm")
    devices = n_space * n_tm
    obs_blocks = observed.shape[0] * n_space // LANES
    tm = lax.axis_index("tm")
    half = (tm // (n_tm // 2)).astype(jnp.int32).reshape(1)

    down = [(i, i + 1) for i in range(n_space - 1)]
    up = [(i + 1, i) for i in range(n_space - 1)]
    before = lax.ppermute(diffusivity[tile_rows - EDGE :], "space", down)
    after = lax.ppermute(diffusivity[:EDGE], "space", up)

    sums, kept = forward(block_count, block_coords, fluxes, footprints, devices, obs_blocks)
    sums = lax.all_to_all(sums, ("space", "tm"), 0, 0, tiled=True)
    share = observed.shape[0] // n_tm
    weight = lax.dynamic_slice_in_dim(obs_weight, tm * share, share)
    target = lax.dynamic_slice_in_dim(observed, tm * share, share)
    misfit, halves = misfit_of(sums, weight, target)
    halves = lax.all_to_all(halves, ("space", "tm"), 0, 0, tiled=True)
    parts = adjoint_of(
        block_count, block_coords, halves, kept, before, diffusivity, after, time_dev
    )
    parts = lax.all_to_all(parts, "tm", 0, 0, tiled=True)
    spill = mix_spill(half, time_cov, parts)
    across = n_tm // 2
    moves = []
    for s in range(n_space):
        for l in range(across):
            if s + 1 < n_space:
                moves.append((s * n_tm + across + l, (s + 1) * n_tm + l))
                moves.append(((s + 1) * n_tm + l, s * n_tm + across + l))
    spill = lax.ppermute(spill, ("space", "tm"), moves)
    mixed = mix(half, time_cov, parts, spill)
    mixed = lax.all_to_all(mixed, "tm", 0, 0, tiled=True)
    field = pl.pallas_call(
        place_kernel,
        out_shape=jax.ShapeDtypeStruct(fluxes.shape, f32),
        name="place",
    )(mixed)
    return misfit.reshape(share), field


def solution(mesh):
    placed = (
        P("tm", "space", None),
        P(("space", "tm"), None, None),
        P(None, ("space", "tm")),
        P(("space", "tm")),
        P("space"),
        P("space"),
        P(),
        P("space", None),
    )
    return jax.shard_map(
        body,
        mesh=mesh,
        in_specs=placed,
        out_specs=(P(("space", "tm")), P("tm", "space", None)),
        check_vma=False,
    )
```

```python
import jax
import jax.numpy as jnp
from jax import lax
from jax.experimental import pallas as pl
from jax.experimental.pallas import tpu as pltpu
from jax.sharding import PartitionSpec as P

SWEEPS = 4
LANES = 128
CHUNKS = 8
EDGE = 8
MIB = 1024 * 1024

f32 = jnp.float32
bf16 = jnp.bfloat16


def split2(x):
    hi = x.astype(bf16)
    return hi, (x - hi.astype(f32)).astype(bf16)


def iota(shape, dim):
    return lax.broadcasted_iota(jnp.int32, shape, dim)


def onehot(equal):
    return jnp.where(equal, 1.0, 0.0).astype(bf16)


def dot(a, b, precision=None):
    return lax.dot_general(
        a, b, (((1,), (0,)), ((), ())), preferred_element_type=f32, precision=precision
    )


def column(row):
    wide = jnp.broadcast_to(row.astype(f32), (LANES, LANES))
    return jnp.transpose(wide, (1, 0)).astype(jnp.int32)


def forward_kernel(tm_ref, count_ref, coords_ref, flux_ref, foot_ref, out_ref, keep_ref, rhs, spread, early, sems):
    slots = foot_ref.shape[0]
    groups = slots // LANES
    per = slots // CHUNKS
    time_dev, tile_rows, width = flux_ref.shape
    across = width // LANES
    steps = time_dev * tile_rows

    def fetch(k):
        part = pl.ds(k * per, per)
        return pltpu.make_async_copy(foot_ref.at[part], keep_ref.at[part], sems.at[k])

    for k in range(CHUNKS):
        fetch(k).start()

    flux = flux_ref[...].reshape(steps, width)
    flux = jnp.concatenate([flux[:, l * LANES : (l + 1) * LANES] for l in range(across)], axis=0)
    lane = iota((LANES, LANES), 1)
    even = (lane & 1) == 0
    for g in range(groups):
        cut = slice(g * LANES, (g + 1) * LANES)
        cell = coords_ref[1:2, cut]
        code = (cell % across) * steps + coords_ref[0:1, cut] * tile_rows + cell // across
        code = column(code)
        pick = jnp.concatenate(
            [onehot(code == lane + j * LANES) for j in range(across * steps // LANES)], axis=1
        )
        piece = jnp.transpose(dot(pick, flux), (1, 0))
        rhs[g, :LANES, :] = jnp.where(even, piece, 0.0).astype(bf16)
        rhs[g, LANES:, :] = jnp.where(even, 0.0, piece).astype(bf16)

    slot = iota((1, slots), 1)
    block = jnp.where(slot < count_ref[0], coords_ref[2:3, :], -1)
    rows = out_ref.shape[0] * out_ref.shape[1]
    cols = out_ref.shape[2] // LANES

    def summed(l, low, high):
        mine = iota((rows, high - low), 0) * cols + l
        full = dot(onehot(mine == block[:, low:high]), spread[low:high, :])
        return full[:, :LANES] + full[:, LANES:]

    pair_of_lane = lane // 2
    chunks_per_group = CHUNKS // groups
    batch = 8
    for g in range(groups):
        total = jnp.zeros((LANES, LANES), f32)
        for part in range(chunks_per_group):
            fetch(g * chunks_per_group + part).wait()
            for i in range(per // (2 * batch)):
                b = g * LANES + part * per + i * 2 * batch
                blocks = keep_ref[b : b + 2 * batch].reshape(batch, 2, LANES, LANES)
                both = jnp.concatenate([blocks[:, 0], blocks[:, 1]], axis=-1)
                result = dot(both.reshape(batch * LANES, 2 * LANES), rhs[g])
                for j in range(batch):
                    p = part * (per // 2) + i * batch + j
                    total = jnp.where(pair_of_lane == p, result[j * LANES : (j + 1) * LANES], total)
        parts = split2(jnp.transpose(total, (1, 0)))
        for n in range(2):
            spread[g * LANES : (g + 1) * LANES, n * LANES : (n + 1) * LANES] = parts[n]
        if g == groups - 2:
            for l in range(cols):
                early[l] = summed(l, 0, slots - LANES)
    for l in range(cols):
        full = early[l] + summed(l, slots - LANES, slots)
        out_ref[:, :, l * LANES : (l + 1) * LANES] = full.reshape(
            out_ref.shape[0], out_ref.shape[1], LANES
        )


def forward(tm, count, coords, fluxes, footprints, devices, obs_blocks):
    per = obs_blocks // devices
    slots = footprints.shape[0]
    cols = per // 4
    vmem = pl.BlockSpec(memory_space=pltpu.VMEM)
    return pl.pallas_call(
        forward_kernel,
        out_shape=(
            jax.ShapeDtypeStruct((devices, 4, cols * LANES), f32),
            pltpu.VMEM(footprints.shape, bf16),
        ),
        in_specs=[
            pl.BlockSpec(memory_space=pltpu.SMEM),
            pl.BlockSpec(memory_space=pltpu.SMEM),
            vmem,
            vmem,
            pl.BlockSpec(memory_space=pltpu.HBM),
        ],
        out_specs=(vmem, vmem),
        scratch_shapes=[
            pltpu.VMEM((slots // LANES, 2 * LANES, LANES), bf16),
            pltpu.VMEM((slots, 2 * LANES), bf16),
            pltpu.VMEM((cols, devices * 4, LANES), f32),
            pltpu.SemaphoreType.DMA((CHUNKS,)),
        ],
        compiler_params=pltpu.CompilerParams(vmem_limit_bytes=38 * MIB),
        name="forward",
    )(tm, count, coords, fluxes, footprints)


def misfit_kernel(tm_ref, sums_ref, weight_ref, observed_ref, out_ref, half_ref):
    devices, quarter, wide = sums_ref.shape
    cols = wide // LANES
    total = jnp.sum(sums_ref[...], axis=0)
    base = tm_ref[0] * (quarter * cols)

    def own(ref):
        return jnp.concatenate(
            [ref[pl.ds(base + l, quarter, stride=cols), :] for l in range(cols)], axis=1
        )

    misfit = own(weight_ref) * (total - own(observed_ref))
    for q in range(quarter):
        for l in range(cols):
            out_ref[q * cols + l : q * cols + l + 1, :] = misfit[
                q : q + 1, l * LANES : (l + 1) * LANES
            ]
    half_ref[...] = jnp.broadcast_to(misfit[None], half_ref.shape).astype(bf16)


def misfit_of(tm, sums, weight, observed):
    devices, quarter, wide = sums.shape
    vmem = pl.BlockSpec(memory_space=pltpu.VMEM)
    return pl.pallas_call(
        misfit_kernel,
        out_shape=(
            jax.ShapeDtypeStruct((quarter * wide // LANES, LANES), f32),
            jax.ShapeDtypeStruct(sums.shape, bf16),
        ),
        in_specs=[pl.BlockSpec(memory_space=pltpu.SMEM), vmem, vmem, vmem],
        out_specs=(vmem, vmem),
        compiler_params=pltpu.CompilerParams(vmem_limit_bytes=4 * MIB),
        name="misfit",
    )(tm, sums, weight.reshape(-1, LANES), observed.reshape(-1, LANES))


def adjoint_kernel(
    count_ref,
    coords_ref,
    misfit_ref,
    foot_ref,
    diff_ref,
    main_ref,
    down_ref,
    up_ref,
    contrib,
    spread,
    rows_ref,
):
    slots = foot_ref.shape[0]
    groups = slots // LANES
    devices, quarter, wide = misfit_ref.shape
    cols = wide // LANES
    rows = devices * quarter
    tile_rows = diff_ref.shape[0]
    lane = iota((LANES, LANES), 1)
    rows_ref[...] = misfit_ref[...].astype(f32).reshape(rows, wide).astype(bf16)
    for g in range(groups):
        block = column(coords_ref[2:3, g * LANES : (g + 1) * LANES])
        chosen = jnp.zeros((LANES, LANES), f32)
        for l in range(cols):
            pick = jnp.concatenate(
                [onehot(block == (lane + j * LANES) * cols + l) for j in range(rows // LANES)], axis=1
            )
            chosen = chosen + dot(pick, rows_ref[:, l * LANES : (l + 1) * LANES])
        contrib[g * LANES : (g + 1) * LANES, :] = chosen

    batch = 16
    sub = iota((batch, LANES), 0)

    def step(i, carry):
        for half in range(2):
            at = pl.multiple_of(i * 2 * batch + half * batch, batch)
            some = contrib[pl.ds(at, batch), :]
            left = jnp.concatenate(
                [jnp.where(sub == j, some, 0.0).astype(bf16) for j in range(batch)], axis=1
            )
            blocks = foot_ref[pl.ds(at, batch)].reshape(batch * LANES, LANES)
            for n, part in enumerate(split2(dot(left, blocks))):
                spread[pl.ds(at, batch), n * LANES : (n + 1) * LANES] = part
        return carry

    lax.fori_loop(0, slots // (2 * batch), step, 0)

    time_dev = main_ref.shape[0] // tile_rows
    width = main_ref.shape[1]
    across = width // LANES
    steps = time_dev * tile_rows
    slot = iota((1, slots), 1)
    cell = coords_ref[1:2, :]
    code = coords_ref[0:1, :] * tile_rows + cell // across
    code = jnp.where(slot < count_ref[0], code, -1)
    for l in range(across):
        cut = slice(l * LANES, (l + 1) * LANES)
        pick = onehot(iota((steps, slots), 0) == jnp.where(cell % across == l, code, -1))
        full = dot(pick, spread[...])
        summed = full[:, :LANES] + full[:, LANES:]
        main_ref[:, cut] = summed.astype(bf16)
        for t in range(time_dev):
            row, at = t * tile_rows, t * SWEEPS
            down_ref[at : at + SWEEPS, cut] = summed[row + tile_rows - SWEEPS : row + tile_rows]
            up_ref[at : at + SWEEPS, cut] = summed[row : row + SWEEPS]
    down_ref[time_dev * SWEEPS :, :] = diff_ref[tile_rows - EDGE :, :]
    up_ref[time_dev * SWEEPS :, :] = diff_ref[:EDGE, :]


def adjoint_of(count, coords, misfit_rows, footprints, diffusivity, time_dev):
    slots = footprints.shape[0]
    tile_rows, width = diffusivity.shape
    devices, quarter, wide = misfit_rows.shape
    vmem = pl.BlockSpec(memory_space=pltpu.VMEM)
    edge = jax.ShapeDtypeStruct((time_dev * SWEEPS + EDGE, width), f32)
    return pl.pallas_call(
        adjoint_kernel,
        out_shape=(jax.ShapeDtypeStruct((time_dev * tile_rows, width), bf16), edge, edge),
        in_specs=[pl.BlockSpec(memory_space=pltpu.SMEM)] + [vmem] * 4,
        out_specs=(vmem, vmem, vmem),
        scratch_shapes=[
            pltpu.VMEM((slots, LANES), f32),
            pltpu.VMEM((slots, 2 * LANES), bf16),
            pltpu.VMEM((devices * quarter, wide), bf16),
        ],
        compiler_params=pltpu.CompilerParams(vmem_limit_bytes=12 * MIB),
        name="adjoint",
    )(count, coords, misfit_rows, footprints, diffusivity)


def mix_kernel(tm_ref, cov_ref, *refs):
    mains, halos, (own_ref, twin_ref) = refs[:4], refs[4:8], refs[8:]
    time_dev, ext_rows, width = own_ref.shape
    tile_rows = ext_rows - EDGE
    times = cov_ref.shape[0]
    depth, core = tm_ref[0] // 2, tm_ref[0] % 2
    block = EDGE * time_dev
    row = iota((2 * block, times), 0)
    core_of = jnp.where(row < block, core, 1 - core)
    tall = (2 * depth + core_of) * time_dev + (row % block) // EDGE == iota((2 * block, times), 1)
    col = iota((times, 4 * block), 1)
    depth_of = (depth + 4 - col // block) % 4
    broad = (2 * depth_of + core) * time_dev + (col % block) // EDGE == iota((times, 4 * block), 0)
    highest = lax.Precision.HIGHEST
    wide = dot(
        dot(onehot(tall).astype(f32), cov_ref[...], highest), onehot(broad).astype(f32), highest
    )
    same = iota(wide.shape, 0) % EDGE == iota(wide.shape, 1) % EDGE
    wide = jnp.concatenate(split2(jnp.where(same, wide, 0.0)), axis=0)

    def mixed(pieces, at):
        full = dot(wide, jnp.concatenate(pieces, axis=0).astype(bf16))
        full = full[: 2 * block] + full[2 * block :]
        for t in range(time_dev):
            own_ref[t, at : at + EDGE, :] = full[t * EDGE : (t + 1) * EDGE]
            twin_ref[t, at : at + EDGE, :] = full[block + t * EDGE : block + (t + 1) * EDGE]

    for r in range(0, tile_rows, EDGE):
        mixed(
            [
                main[u * tile_rows + r : u * tile_rows + r + EDGE, :].astype(f32)
                for main in mains
                for u in range(time_dev)
            ],
            r,
        )
    pieces = []
    for halo in halos:
        edges = halo[...].astype(f32)
        for u in range(time_dev):
            for n in (u, u + time_dev):
                pieces.append(edges[n * SWEEPS : (n + 1) * SWEEPS])
    mixed(pieces, tile_rows)


def mix(tm, cov, mains, halos, shape):
    vmem = pl.BlockSpec(memory_space=pltpu.VMEM)
    whole = jax.ShapeDtypeStruct((shape[0], shape[1] + EDGE, shape[2]), f32)
    return pl.pallas_call(
        mix_kernel,
        out_shape=(whole, whole),
        in_specs=[pl.BlockSpec(memory_space=pltpu.SMEM)] + [vmem] * 9,
        out_specs=(vmem, vmem),
        compiler_params=pltpu.CompilerParams(vmem_limit_bytes=8 * MIB),
        name="mix",
    )(tm, cov, *mains, *halos)


def diffuse_kernel(own_ref, twin_ref, before_ref, diff_ref, after_ref, out_ref, field, other):
    time_dev, tile_rows, width = out_ref.shape
    ext_rows = field.shape[1]
    first, last = 2 * EDGE, 2 * EDGE + tile_rows
    edge = before_ref.shape[0] - EDGE
    diff = jnp.concatenate([before_ref[edge:, :], diff_ref[...], after_ref[edge:, :]], axis=0)
    column_of = iota(diff.shape, 1)
    here = slice(EDGE, ext_rows - EDGE)
    for buffer in (field, other):
        for t in range(time_dev):
            buffer[t, :first, :] = jnp.zeros((first, width), f32)
            buffer[t, last:, :] = jnp.zeros((ext_rows - last, width), f32)
    for t in range(time_dev):
        field[t, first:last, :] = own_ref[t, :tile_rows, :] + twin_ref[t, :tile_rows, :]
        halo = own_ref[t, tile_rows:, :] + twin_ref[t, tile_rows:, :]
        field[t, first - SWEEPS : first, :] = halo[:SWEEPS]
        field[t, last : last + SWEEPS, :] = halo[SWEEPS:]
    source, target = field, other
    for sweep in range(SWEEPS):
        for t in range(time_dev):
            centre = source[t, here, :]
            left = jnp.where(column_of == 0, 0.0, pltpu.roll(centre, 1, 1))
            right = jnp.where(column_of == width - 1, 0.0, pltpu.roll(centre, width - 1, 1))
            above = source[t, EDGE - 1 : ext_rows - EDGE - 1, :]
            below = source[t, EDGE + 1 : ext_rows - EDGE + 1, :]
            moved = centre + diff * (below + above + right + left - 4.0 * centre)
            if sweep + 1 < SWEEPS:
                target[t, here, :] = moved
            else:
                out_ref[t] = moved[EDGE : EDGE + tile_rows]
        source, target = target, source


def diffuse(own, twin, before, diffusivity, after):
    time_dev = own.shape[0]
    tile_rows, width = diffusivity.shape
    field = pltpu.VMEM((time_dev, tile_rows + 4 * EDGE, width), f32)
    vmem = pl.BlockSpec(memory_space=pltpu.VMEM)
    return pl.pallas_call(
        diffuse_kernel,
        out_shape=jax.ShapeDtypeStruct((time_dev, tile_rows, width), f32),
        in_specs=[vmem] * 5,
        out_specs=vmem,
        scratch_shapes=[field, field],
        compiler_params=pltpu.CompilerParams(vmem_limit_bytes=8 * MIB),
        name="diffuse",
    )(own, twin, before, diffusivity, after)


def body(
    fluxes, footprints, block_coords, block_count, observed, obs_weight, time_cov, diffusivity
):
    time_dev, tile_rows, width = fluxes.shape
    n_space, n_tm = lax.axis_size("space"), lax.axis_size("tm")
    devices = n_space * n_tm
    obs_blocks = observed.shape[0] * n_space // LANES
    tm = lax.axis_index("tm").astype(jnp.int32).reshape(1)
    both = ("space", "tm")

    sums, kept = forward(tm, block_count, block_coords, fluxes, footprints, devices, obs_blocks)
    sums = lax.all_to_all(sums, both, 0, 0, tiled=True)
    misfit, halves = misfit_of(tm, sums, obs_weight, observed)
    halves = lax.all_to_all(halves, both, 0, 0, tiled=True)
    main, edge_down, edge_up = adjoint_of(
        block_count, block_coords, halves, kept, diffusivity, time_dev
    )

    def along(array, steps):
        return lax.ppermute(array, "tm", [(i, (i + 2 * steps) % n_tm) for i in range(n_tm)])

    mains = [main] + [along(main, k) for k in (1, 2, 3)]
    before = lax.ppermute(edge_down, "space", [(i, i + 1) for i in range(n_space - 1)])
    after = lax.ppermute(edge_up, "space", [(i + 1, i) for i in range(n_space - 1)])
    field_rows = time_dev * SWEEPS
    halo = jnp.concatenate([before[:field_rows], after[:field_rows]], axis=0).astype(bf16)
    halos = [halo] + [along(halo, k) for k in (1, 2, 3)]
    own, twin = mix(tm, time_cov, mains, halos, fluxes.shape)
    twin = lax.ppermute(twin, "tm", [(i, i ^ 1) for i in range(n_tm)])
    gradient = diffuse(own, twin, before, diffusivity, after)
    return misfit.reshape(-1), gradient


def solution(mesh):
    placed = (
        P("tm", "space", None),
        P(("space", "tm"), None, None),
        P(None, ("space", "tm")),
        P(("space", "tm")),
        P("space"),
        P("space"),
        P(),
        P("space", None),
    )
    return jax.shard_map(
        body,
        mesh=mesh,
        in_specs=placed,
        out_specs=(P(("space", "tm")), P("tm", "space", None)),
        check_vma=False,
    )
```

```python
import jax
import jax.numpy as jnp
from jax import lax
from jax.experimental import pallas as pl
from jax.experimental.pallas import tpu as pltpu
from jax.sharding import PartitionSpec as P

SWEEPS = 4
LANES = 128
EDGE = 8
MIB = 1024 * 1024

f32 = jnp.float32
bf16 = jnp.bfloat16


def split2(x):
    hi = x.astype(bf16)
    return hi, (x - hi.astype(f32)).astype(bf16)


def iota(shape, dim):
    return lax.broadcasted_iota(jnp.int32, shape, dim)


def onehot(equal):
    return jnp.where(equal, 1.0, 0.0).astype(bf16)


def dot(a, b, precision=None):
    return lax.dot_general(
        a, b, (((1,), (0,)), ((), ())), preferred_element_type=f32, precision=precision
    )


def column(row):
    wide = jnp.broadcast_to(row.astype(f32), (LANES, LANES))
    return jnp.transpose(wide, (1, 0)).astype(jnp.int32)


def forward_kernel(
    tm_ref,
    count_ref,
    coords_hbm,
    flux_hbm,
    foot_ref,
    out_ref,
    keep_ref,
    coords_ref,
    flux_ref,
    rhs,
    spread,
    early,
    sems,
    small_sems,
):
    slots = foot_ref.shape[0]
    groups = slots // LANES
    time_dev, tile_rows, width = flux_ref.shape
    across = width // LANES
    steps = time_dev * tile_rows
    bounds = [0] + list(range(LANES // 2, slots, LANES)) + [slots]
    chunks = len(bounds) - 1

    def fetch(k):
        part = pl.ds(bounds[k], bounds[k + 1] - bounds[k])
        return pltpu.make_async_copy(foot_ref.at[part], keep_ref.at[part], sems.at[k])

    small = (
        pltpu.make_async_copy(coords_hbm, coords_ref, small_sems.at[0]),
        pltpu.make_async_copy(flux_hbm, flux_ref, small_sems.at[1]),
    )
    for copy in small:
        copy.start()
    fetch(0).start()
    fetch(1).start()
    for copy in small:
        copy.wait()

    flux = flux_ref[...].reshape(steps, width)
    flux = jnp.concatenate([flux[:, l * LANES : (l + 1) * LANES] for l in range(across)], axis=0)
    lane = iota((LANES, LANES), 1)
    even = (lane & 1) == 0
    for g in range(groups):
        cut = slice(g * LANES, (g + 1) * LANES)
        cell = coords_ref[1:2, cut]
        code = (cell % across) * steps + coords_ref[0:1, cut] * tile_rows + cell // across
        code = column(code)
        pick = jnp.concatenate(
            [onehot(code == lane + j * LANES) for j in range(across * steps // LANES)], axis=1
        )
        piece = jnp.transpose(dot(pick, flux), (1, 0))
        rhs[g, :LANES, :] = jnp.where(even, piece, 0.0).astype(bf16)
        rhs[g, LANES:, :] = jnp.where(even, 0.0, piece).astype(bf16)

    slot = iota((1, slots), 1)
    block = jnp.where(slot < count_ref[0], coords_ref[2:3, :], -1)
    rows = out_ref.shape[0] * out_ref.shape[1]
    cols = out_ref.shape[2] // LANES

    def summed(l, low, high):
        mine = iota((rows, high - low), 0) * cols + l
        full = dot(onehot(mine == block[:, low:high]), spread[low:high, :])
        return full[:, :LANES] + full[:, LANES:]

    pair_of_lane = lane // 2
    batch = 8
    total = None
    for k in range(chunks):
        fetch(k).wait()
        if k + 2 < chunks:
            fetch(k + 2).start()
        for b in range(bounds[k], bounds[k + 1], 2 * batch):
            g = b // LANES
            if b % LANES == 0:
                total = jnp.zeros((LANES, LANES), f32)
            blocks = keep_ref[b : b + 2 * batch].reshape(batch, 2, LANES, LANES)
            both = jnp.concatenate([blocks[:, 0], blocks[:, 1]], axis=-1)
            result = dot(both.reshape(batch * LANES, 2 * LANES), rhs[g])
            for j in range(batch):
                p = (b % LANES) // 2 + j
                total = jnp.where(pair_of_lane == p, result[j * LANES : (j + 1) * LANES], total)
            if (b + 2 * batch) % LANES == 0:
                for n, part in enumerate(split2(jnp.transpose(total, (1, 0)))):
                    spread[g * LANES : (g + 1) * LANES, n * LANES : (n + 1) * LANES] = part
                if g == groups - 2:
                    for l in range(cols):
                        early[l] = summed(l, 0, slots - LANES)
    for l in range(cols):
        full = early[l] + summed(l, slots - LANES, slots)
        out_ref[:, :, l * LANES : (l + 1) * LANES] = full.reshape(
            out_ref.shape[0], out_ref.shape[1], LANES
        )


def forward(tm, count, coords, fluxes, footprints, devices, obs_blocks):
    per = obs_blocks // devices
    slots = footprints.shape[0]
    cols = per // 4
    vmem = pl.BlockSpec(memory_space=pltpu.VMEM)
    smem = pl.BlockSpec(memory_space=pltpu.SMEM)
    hbm = pl.BlockSpec(memory_space=pltpu.HBM)
    return pl.pallas_call(
        forward_kernel,
        out_shape=(
            pltpu.VMEM((devices, 4, cols * LANES), f32),
            pltpu.VMEM(footprints.shape, bf16),
        ),
        in_specs=[smem, smem, hbm, hbm, hbm],
        out_specs=(vmem, vmem),
        scratch_shapes=[
            pltpu.VMEM(coords.shape, jnp.int32),
            pltpu.VMEM(fluxes.shape, bf16),
            pltpu.VMEM((slots // LANES, 2 * LANES, LANES), bf16),
            pltpu.VMEM((slots, 2 * LANES), bf16),
            pltpu.VMEM((cols, devices * 4, LANES), f32),
            pltpu.SemaphoreType.DMA((slots // LANES + 1,)),
            pltpu.SemaphoreType.DMA((2,)),
        ],
        compiler_params=pltpu.CompilerParams(vmem_limit_bytes=38 * MIB),
        name="forward",
    )(tm, count, coords, fluxes, footprints)


def misfit_kernel(tm_ref, sums_ref, weight_ref, observed_ref, out_ref, half_ref):
    devices, quarter, wide = sums_ref.shape
    cols = wide // LANES
    total = jnp.sum(sums_ref[...], axis=0)
    base = tm_ref[0] * (quarter * cols)

    def own(ref):
        return jnp.concatenate(
            [ref[pl.ds(base + l, quarter, stride=cols), :] for l in range(cols)], axis=1
        )

    misfit = own(weight_ref) * (total - own(observed_ref))
    for q in range(quarter):
        for l in range(cols):
            out_ref[q * cols + l : q * cols + l + 1, :] = misfit[
                q : q + 1, l * LANES : (l + 1) * LANES
            ]
    half_ref[...] = jnp.broadcast_to(misfit[None], half_ref.shape).astype(bf16)


def misfit_of(tm, sums, weight, observed):
    devices, quarter, wide = sums.shape
    vmem = pl.BlockSpec(memory_space=pltpu.VMEM)
    return pl.pallas_call(
        misfit_kernel,
        out_shape=(
            jax.ShapeDtypeStruct((quarter * wide // LANES, LANES), f32),
            jax.ShapeDtypeStruct(sums.shape, bf16),
        ),
        in_specs=[pl.BlockSpec(memory_space=pltpu.SMEM), vmem, vmem, vmem],
        out_specs=(vmem, vmem),
        compiler_params=pltpu.CompilerParams(vmem_limit_bytes=4 * MIB),
        name="misfit",
    )(tm, sums, weight.reshape(-1, LANES), observed.reshape(-1, LANES))


def adjoint_kernel(
    tm_ref,
    count_ref,
    coords_ref,
    misfit_ref,
    foot_ref,
    diff_ref,
    main_ref,
    mine_ref,
    other_ref,
    contrib,
    spread,
    rows_ref,
):
    slots = foot_ref.shape[0]
    groups = slots // LANES
    devices, quarter, wide = misfit_ref.shape
    cols = wide // LANES
    rows = devices * quarter
    tile_rows = diff_ref.shape[0]
    lane = iota((LANES, LANES), 1)
    rows_ref[...] = misfit_ref[...].astype(f32).reshape(rows, wide).astype(bf16)
    for g in range(groups):
        block = column(coords_ref[2:3, g * LANES : (g + 1) * LANES])
        chosen = jnp.zeros((LANES, LANES), f32)
        for l in range(cols):
            pick = jnp.concatenate(
                [onehot(block == (lane + j * LANES) * cols + l) for j in range(rows // LANES)], axis=1
            )
            chosen = chosen + dot(pick, rows_ref[:, l * LANES : (l + 1) * LANES])
        contrib[g * LANES : (g + 1) * LANES, :] = chosen

    batch = 16
    sub = iota((batch, LANES), 0)
    for at in range(0, slots, batch):
        some = contrib[at : at + batch, :]
        left = jnp.concatenate(
            [jnp.where(sub == j, some, 0.0).astype(bf16) for j in range(batch)], axis=1
        )
        blocks = foot_ref[at : at + batch].reshape(batch * LANES, LANES)
        for n, part in enumerate(split2(dot(left, blocks))):
            spread[at : at + batch, n * LANES : (n + 1) * LANES] = part

    time_dev = main_ref.shape[0] // tile_rows
    width = main_ref.shape[1]
    across = width // LANES
    steps = time_dev * tile_rows
    first_core = tm_ref[0] % 2 == 0
    slot = iota((1, slots), 1)
    cell = coords_ref[1:2, :]
    code = coords_ref[0:1, :] * tile_rows + cell // across
    code = jnp.where(slot < count_ref[0], code, -1)
    for l in range(across):
        cut = slice(l * LANES, (l + 1) * LANES)
        pick = onehot(iota((steps, slots), 0) == jnp.where(cell % across == l, code, -1))
        full = dot(pick, spread[...])
        summed = full[:, :LANES] + full[:, LANES:]
        main_ref[:, cut] = summed.astype(bf16)
        for t in range(time_dev):
            row, at = t * tile_rows, t * SWEEPS
            down = summed[row + tile_rows - SWEEPS : row + tile_rows]
            up = summed[row : row + SWEEPS]
            mine_ref[at : at + SWEEPS, cut] = jnp.where(first_core, down, up)
            other_ref[at : at + SWEEPS, cut] = jnp.where(first_core, up, down)
    mine_ref[time_dev * SWEEPS :, :] = jnp.where(
        first_core, diff_ref[tile_rows - EDGE :, :], diff_ref[:EDGE, :]
    )


def adjoint_of(tm, count, coords, misfit_rows, footprints, diffusivity, time_dev):
    slots = footprints.shape[0]
    tile_rows, width = diffusivity.shape
    devices, quarter, wide = misfit_rows.shape
    edge = time_dev * SWEEPS
    vmem = pl.BlockSpec(memory_space=pltpu.VMEM)
    smem = pl.BlockSpec(memory_space=pltpu.SMEM)
    return pl.pallas_call(
        adjoint_kernel,
        out_shape=(
            jax.ShapeDtypeStruct((time_dev * tile_rows, width), bf16),
            jax.ShapeDtypeStruct((edge + EDGE, width), f32),
            jax.ShapeDtypeStruct((edge, width), f32),
        ),
        in_specs=[smem, smem, vmem, vmem, vmem, vmem],
        out_specs=(vmem, vmem, vmem),
        scratch_shapes=[
            pltpu.VMEM((slots, LANES), f32),
            pltpu.VMEM((slots, 2 * LANES), bf16),
            pltpu.VMEM((devices * quarter, wide), bf16),
        ],
        compiler_params=pltpu.CompilerParams(vmem_limit_bytes=12 * MIB),
        name="adjoint",
    )(tm, count, coords, misfit_rows, footprints, diffusivity)


def spread_cov(cov, row_time, col_time, per):
    times = cov.shape[0]
    rows, cols = row_time.shape[0], col_time.shape[1]
    tall = onehot(row_time == iota((rows, times), 1)).astype(f32)
    broad = onehot(col_time == iota((times, cols), 0)).astype(f32)
    highest = lax.Precision.HIGHEST
    wide = dot(dot(tall, cov, highest), broad, highest)
    same = iota((rows, cols), 0) % per == iota((rows, cols), 1) % per
    return jnp.concatenate(split2(jnp.where(same, wide, 0.0)), axis=0)


def mix_kernel(tm_ref, cov_ref, *refs):
    mains, halos, received_ref, (own_ref, twin_ref) = refs[:4], refs[4:8], refs[8], refs[9:]
    time_dev, ext_rows, width = own_ref.shape
    tile_rows = ext_rows - EDGE
    times = cov_ref.shape[0]
    depth, core = tm_ref[0] // 2, tm_ref[0] % 2

    def target_time(per):
        row = iota((2 * time_dev * per, times), 0)
        core_of = jnp.where(row < time_dev * per, core, 1 - core)
        return (2 * depth + core_of) * time_dev + row % (time_dev * per) // per

    def depth_of(col, block):
        return (depth + 4 - col // block) % 4

    def put(full, at, count):
        half = full.shape[0] // 2
        full = full[:half] + full[half:]
        for t in range(time_dev):
            row = t * count
            own_ref[t, at : at + count, :] = full[row : row + count]
            row += time_dev * count
            twin_ref[t, at : at + count, :] = full[row : row + count]

    block = EDGE * time_dev
    col = iota((times, 4 * block), 1)
    source = (2 * depth_of(col, block) + core) * time_dev + col % block // EDGE
    wide = spread_cov(cov_ref[...], target_time(EDGE), source, EDGE)
    for r in range(0, tile_rows, EDGE):
        pieces = [
            main[u * tile_rows + r : u * tile_rows + r + EDGE, :].astype(f32)
            for main in mains
            for u in range(time_dev)
        ]
        put(dot(wide, jnp.concatenate(pieces, axis=0).astype(bf16)), r, EDGE)

    half = SWEEPS * time_dev
    col = iota((times, 8 * half), 1)
    core_of = jnp.where(col % (2 * half) < half, 1 - core, core)
    source = (2 * depth_of(col, 2 * half) + core_of) * time_dev + col % half // SWEEPS
    wide = spread_cov(cov_ref[...], target_time(SWEEPS), source, SWEEPS)
    edges = jnp.concatenate([halo[...] for halo in halos], axis=0)
    put(dot(wide, edges), tile_rows, SWEEPS)
    for t in range(time_dev):
        n = 2 * half + (t % 2) * SWEEPS
        for ref in (own_ref, twin_ref):
            ref[t, tile_rows + SWEEPS :, :] = received_ref[n : n + SWEEPS, :]


def mix(tm, cov, mains, halos, received, shape):
    vmem = pl.BlockSpec(memory_space=pltpu.VMEM)
    whole = jax.ShapeDtypeStruct((shape[0], shape[1] + EDGE, shape[2]), f32)
    return pl.pallas_call(
        mix_kernel,
        out_shape=(whole, whole),
        in_specs=[pl.BlockSpec(memory_space=pltpu.SMEM)] + [vmem] * 10,
        out_specs=(vmem, vmem),
        compiler_params=pltpu.CompilerParams(vmem_limit_bytes=8 * MIB),
        name="mix",
    )(tm, cov, *mains, *halos, received)


def diffuse_kernel(tm_ref, own_ref, twin_ref, diff_ref, out_ref, field, other):
    time_dev, tile_rows, width = out_ref.shape
    ext_rows = field.shape[1]
    first, last = 2 * EDGE, 2 * EDGE + tile_rows
    first_core = tm_ref[0] % 2 == 0
    lower = tile_rows + SWEEPS

    def halo_of(ref):
        return jnp.concatenate([ref[0, lower:, :], ref[1, lower:, :]], axis=0)

    def ordered(a, b):
        return jnp.where(first_core, a, b), jnp.where(first_core, b, a)

    before, after = ordered(halo_of(own_ref), halo_of(twin_ref))
    diff = jnp.concatenate([before, diff_ref[...], after], axis=0)
    column_of = iota(diff.shape, 1)
    here = slice(EDGE, ext_rows - EDGE)
    for buffer in (field, other):
        for t in range(time_dev):
            buffer[t, :first, :] = jnp.zeros((first, width), f32)
            buffer[t, last:, :] = jnp.zeros((ext_rows - last, width), f32)
    for t in range(time_dev):
        field[t, first:last, :] = own_ref[t, :tile_rows, :] + twin_ref[t, :tile_rows, :]
        above, below = ordered(own_ref[t, tile_rows:lower, :], twin_ref[t, tile_rows:lower, :])
        field[t, first - SWEEPS : first, :] = above
        field[t, last : last + SWEEPS, :] = below
    source, target = field, other
    for sweep in range(SWEEPS):
        for t in range(time_dev):
            centre = source[t, here, :]
            left = jnp.where(column_of == 0, 0.0, pltpu.roll(centre, 1, 1))
            right = jnp.where(column_of == width - 1, 0.0, pltpu.roll(centre, width - 1, 1))
            above = source[t, EDGE - 1 : ext_rows - EDGE - 1, :]
            below = source[t, EDGE + 1 : ext_rows - EDGE + 1, :]
            moved = centre + diff * (below + above + right + left - 4.0 * centre)
            if sweep + 1 < SWEEPS:
                target[t, here, :] = moved
            else:
                out_ref[t] = moved[EDGE : EDGE + tile_rows]
        source, target = target, source


def diffuse(tm, own, twin, diffusivity):
    time_dev = own.shape[0]
    tile_rows, width = diffusivity.shape
    field = pltpu.VMEM((time_dev, tile_rows + 4 * EDGE, width), f32)
    vmem = pl.BlockSpec(memory_space=pltpu.VMEM)
    return pl.pallas_call(
        diffuse_kernel,
        out_shape=jax.ShapeDtypeStruct((time_dev, tile_rows, width), f32),
        in_specs=[pl.BlockSpec(memory_space=pltpu.SMEM)] + [vmem] * 3,
        out_specs=vmem,
        scratch_shapes=[field, field],
        compiler_params=pltpu.CompilerParams(vmem_limit_bytes=8 * MIB),
        name="diffuse",
    )(tm, own, twin, diffusivity)


def body(
    fluxes, footprints, block_coords, block_count, observed, obs_weight, time_cov, diffusivity
):
    time_dev, tile_rows, width = fluxes.shape
    n_space, n_tm = lax.axis_size("space"), lax.axis_size("tm")
    devices = n_space * n_tm
    obs_blocks = observed.shape[0] * n_space // LANES
    tm = lax.axis_index("tm").astype(jnp.int32).reshape(1)
    both = ("space", "tm")

    sums, kept = forward(tm, block_count, block_coords, fluxes, footprints, devices, obs_blocks)
    sums = lax.all_to_all(sums, both, 0, 0, tiled=True)
    misfit, halves = misfit_of(tm, sums, obs_weight, observed)
    halves = lax.all_to_all(halves, both, 0, 0, tiled=True)
    main, mine, other = adjoint_of(
        tm, block_count, block_coords, halves, kept, diffusivity, time_dev
    )

    def along(array, steps):
        return lax.ppermute(array, "tm", [(i, (i + 2 * steps) % n_tm) for i in range(n_tm)])

    swap = [(i, i ^ 1) for i in range(n_tm)]
    other = lax.ppermute(other, "tm", swap)
    mains = [main] + [along(main, k) for k in (1, 2, 3)]
    moves = []
    for s in range(n_space - 1):
        for t in range(0, n_tm, 2):
            moves.append((s * n_tm + t, (s + 1) * n_tm + t))
            moves.append(((s + 1) * n_tm + t + 1, s * n_tm + t + 1))
    received = lax.ppermute(jnp.concatenate([other, mine], axis=0), both, moves)
    halo = received[: 2 * time_dev * SWEEPS].astype(bf16)
    halo, mains[3] = lax.optimization_barrier((halo, mains[3]))
    halos = [halo] + [along(halo, k) for k in (1, 2, 3)]
    own, twin = mix(tm, time_cov, mains, halos, received, fluxes.shape)
    twin = lax.ppermute(twin, "tm", swap)
    gradient = diffuse(tm, own, twin, diffusivity)
    return misfit.reshape(-1), gradient


def solution(mesh):
    placed = (
        P("tm", "space", None),
        P(("space", "tm"), None, None),
        P(None, ("space", "tm")),
        P(("space", "tm")),
        P("space"),
        P("space"),
        P(),
        P("space", None),
    )
    return jax.shard_map(
        body,
        mesh=mesh,
        in_specs=placed,
        out_specs=(P(("space", "tm")), P("tm", "space", None)),
        check_vma=False,
    )
```

```python
import jax
import jax.numpy as jnp
from jax import lax
from jax.experimental import pallas as pl
from jax.experimental.pallas import tpu as pltpu
from jax.sharding import PartitionSpec as P

SWEEPS = 4
LANES = 128
EDGE = 8
MIB = 1024 * 1024

f32 = jnp.float32
bf16 = jnp.bfloat16


def split2(x):
    hi = x.astype(bf16)
    return hi, (x - hi.astype(f32)).astype(bf16)


def iota(shape, dim):
    return lax.broadcasted_iota(jnp.int32, shape, dim)


def onehot(equal):
    return jnp.where(equal, 1.0, 0.0).astype(bf16)


def dot(a, b, precision=None):
    return lax.dot_general(
        a, b, (((1,), (0,)), ((), ())), preferred_element_type=f32, precision=precision
    )


def column(row):
    wide = jnp.broadcast_to(row.astype(f32), (LANES, LANES))
    return jnp.transpose(wide, (1, 0)).astype(jnp.int32)


def forward_kernel(
    tm_ref,
    count_ref,
    coords_hbm,
    flux_hbm,
    foot_ref,
    mine_ref,
    other_ref,
    keep_ref,
    coords_ref,
    flux_ref,
    rhs,
    spread,
    early,
    sems,
    small_sems,
):
    slots = foot_ref.shape[0]
    groups = slots // LANES
    time_dev, tile_rows, width = flux_ref.shape
    across = width // LANES
    steps = time_dev * tile_rows
    bounds = [0] + list(range(LANES // 2, slots, LANES)) + [slots]
    chunks = len(bounds) - 1

    def fetch(k):
        part = pl.ds(bounds[k], bounds[k + 1] - bounds[k])
        return pltpu.make_async_copy(foot_ref.at[part], keep_ref.at[part], sems.at[k])

    small = (
        pltpu.make_async_copy(coords_hbm, coords_ref, small_sems.at[0]),
        pltpu.make_async_copy(flux_hbm, flux_ref, small_sems.at[1]),
    )
    for copy in small:
        copy.start()
    fetch(0).start()
    fetch(1).start()
    for copy in small:
        copy.wait()

    flux = flux_ref[...].reshape(steps, width)
    flux = jnp.concatenate([flux[:, l * LANES : (l + 1) * LANES] for l in range(across)], axis=0)
    lane = iota((LANES, LANES), 1)
    even = (lane & 1) == 0
    for g in range(groups):
        cut = slice(g * LANES, (g + 1) * LANES)
        cell = coords_ref[1:2, cut]
        code = (cell % across) * steps + coords_ref[0:1, cut] * tile_rows + cell // across
        code = column(code)
        pick = jnp.concatenate(
            [onehot(code == lane + j * LANES) for j in range(across * steps // LANES)], axis=1
        )
        piece = jnp.transpose(dot(pick, flux), (1, 0))
        rhs[g, :LANES, :] = jnp.where(even, piece, 0.0).astype(bf16)
        rhs[g, LANES:, :] = jnp.where(even, 0.0, piece).astype(bf16)

    slot = iota((1, slots), 1)
    block = jnp.where(slot < count_ref[0], coords_ref[2:3, :], -1)
    chips, quarter, wide = mine_ref.shape
    cols = wide // LANES
    core = tm_ref[0] % 2

    def summed(n, low, high):
        row = iota((chips * quarter, high - low), 0)
        owner = row // quarter * 2 + (core if n < cols else 1 - core)
        row = (owner * quarter + row % quarter) * cols + n % cols
        full = dot(onehot(row == block[:, low:high]), spread[low:high, :])
        return full[:, :LANES] + full[:, LANES:]

    pair_of_lane = lane // 2
    batch = 8
    total = None
    for k in range(chunks):
        fetch(k).wait()
        if k + 2 < chunks:
            fetch(k + 2).start()
        for b in range(bounds[k], bounds[k + 1], 2 * batch):
            g = b // LANES
            if b % LANES == 0:
                total = jnp.zeros((LANES, LANES), f32)
            blocks = keep_ref[b : b + 2 * batch].reshape(batch, 2, LANES, LANES)
            both = jnp.concatenate([blocks[:, 0], blocks[:, 1]], axis=-1)
            result = dot(both.reshape(batch * LANES, 2 * LANES), rhs[g])
            for j in range(batch):
                p = (b % LANES) // 2 + j
                total = jnp.where(pair_of_lane == p, result[j * LANES : (j + 1) * LANES], total)
            if (b + 2 * batch) % LANES == 0:
                for n, part in enumerate(split2(jnp.transpose(total, (1, 0)))):
                    spread[g * LANES : (g + 1) * LANES, n * LANES : (n + 1) * LANES] = part
                if g == groups - 2:
                    for n in range(2 * cols):
                        early[n] = summed(n, 0, slots - LANES)
    for n in range(2 * cols):
        full = early[n] + summed(n, slots - LANES, slots)
        ref = mine_ref if n < cols else other_ref
        ref[:, :, n % cols * LANES : (n % cols + 1) * LANES] = full.reshape(chips, quarter, LANES)


def forward(tm, count, coords, fluxes, footprints, devices, obs_blocks):
    per = obs_blocks // devices
    slots = footprints.shape[0]
    cols = per // 4
    vmem = pl.BlockSpec(memory_space=pltpu.VMEM)
    smem = pl.BlockSpec(memory_space=pltpu.SMEM)
    hbm = pl.BlockSpec(memory_space=pltpu.HBM)
    return pl.pallas_call(
        forward_kernel,
        out_shape=(
            pltpu.VMEM((devices // 2, 4, cols * LANES), f32),
            pltpu.VMEM((devices // 2, 4, cols * LANES), f32),
            pltpu.VMEM(footprints.shape, bf16),
        ),
        in_specs=[smem, smem, hbm, hbm, hbm],
        out_specs=(vmem, vmem, vmem),
        scratch_shapes=[
            pltpu.VMEM(coords.shape, jnp.int32),
            pltpu.VMEM(fluxes.shape, bf16),
            pltpu.VMEM((slots // LANES, 2 * LANES, LANES), bf16),
            pltpu.VMEM((slots, 2 * LANES), bf16),
            pltpu.VMEM((2 * cols, devices * 2, LANES), f32),
            pltpu.SemaphoreType.DMA((slots // LANES + 1,)),
            pltpu.SemaphoreType.DMA((2,)),
        ],
        compiler_params=pltpu.CompilerParams(vmem_limit_bytes=38 * MIB),
        name="forward",
    )(tm, count, coords, fluxes, footprints)


def misfit_kernel(tm_ref, sums_ref, weight_ref, observed_ref, out_ref, half_ref):
    devices, quarter, wide = sums_ref.shape
    cols = wide // LANES
    total = jnp.sum(sums_ref[...], axis=0)
    base = tm_ref[0] * (quarter * cols)

    def own(ref):
        return jnp.concatenate(
            [ref[pl.ds(base + l, quarter, stride=cols), :] for l in range(cols)], axis=1
        )

    misfit = own(weight_ref) * (total - own(observed_ref))
    for q in range(quarter):
        for l in range(cols):
            out_ref[q * cols + l : q * cols + l + 1, :] = misfit[
                q : q + 1, l * LANES : (l + 1) * LANES
            ]
    half_ref[...] = jnp.broadcast_to(misfit[None], half_ref.shape).astype(bf16)


def misfit_of(tm, sums, weight, observed):
    devices, quarter, wide = sums.shape
    vmem = pl.BlockSpec(memory_space=pltpu.VMEM)
    return pl.pallas_call(
        misfit_kernel,
        out_shape=(
            jax.ShapeDtypeStruct((quarter * wide // LANES, LANES), f32),
            jax.ShapeDtypeStruct((2 * devices, quarter, wide), bf16),
        ),
        in_specs=[pl.BlockSpec(memory_space=pltpu.SMEM), vmem, vmem, vmem],
        out_specs=(vmem, vmem),
        compiler_params=pltpu.CompilerParams(vmem_limit_bytes=4 * MIB),
        name="misfit",
    )(tm, sums, weight.reshape(-1, LANES), observed.reshape(-1, LANES))


def adjoint_kernel(
    tm_ref,
    count_ref,
    coords_ref,
    misfit_ref,
    foot_ref,
    diff_ref,
    main_ref,
    mine_ref,
    other_ref,
    contrib,
    spread,
    rows_ref,
):
    slots = foot_ref.shape[0]
    groups = slots // LANES
    devices, quarter, wide = misfit_ref.shape
    cols = wide // LANES
    rows = devices * quarter
    tile_rows = diff_ref.shape[0]
    lane = iota((LANES, LANES), 1)
    rows_ref[...] = misfit_ref[...].astype(f32).reshape(rows, wide).astype(bf16)
    for g in range(groups):
        block = column(coords_ref[2:3, g * LANES : (g + 1) * LANES])
        chosen = jnp.zeros((LANES, LANES), f32)
        for l in range(cols):
            pick = jnp.concatenate(
                [onehot(block == (lane + j * LANES) * cols + l) for j in range(rows // LANES)], axis=1
            )
            chosen = chosen + dot(pick, rows_ref[:, l * LANES : (l + 1) * LANES])
        contrib[g * LANES : (g + 1) * LANES, :] = chosen

    batch = 16
    sub = iota((batch, LANES), 0)
    for at in range(0, slots, batch):
        some = contrib[at : at + batch, :]
        left = jnp.concatenate(
            [jnp.where(sub == j, some, 0.0).astype(bf16) for j in range(batch)], axis=1
        )
        blocks = foot_ref[at : at + batch].reshape(batch * LANES, LANES)
        for n, part in enumerate(split2(dot(left, blocks))):
            spread[at : at + batch, n * LANES : (n + 1) * LANES] = part

    time_dev = main_ref.shape[0] // tile_rows
    width = main_ref.shape[1]
    across = width // LANES
    steps = time_dev * tile_rows
    first_core = tm_ref[0] % 2 == 0
    slot = iota((1, slots), 1)
    cell = coords_ref[1:2, :]
    code = coords_ref[0:1, :] * tile_rows + cell // across
    code = jnp.where(slot < count_ref[0], code, -1)
    for l in range(across):
        cut = slice(l * LANES, (l + 1) * LANES)
        pick = onehot(iota((steps, slots), 0) == jnp.where(cell % across == l, code, -1))
        full = dot(pick, spread[...])
        summed = full[:, :LANES] + full[:, LANES:]
        main_ref[:, cut] = summed.astype(bf16)
        for t in range(time_dev):
            row, at = t * tile_rows, t * SWEEPS
            down = summed[row + tile_rows - SWEEPS : row + tile_rows]
            up = summed[row : row + SWEEPS]
            mine_ref[at : at + SWEEPS, cut] = jnp.where(first_core, down, up)
            other_ref[at : at + SWEEPS, cut] = jnp.where(first_core, up, down)
    mine_ref[time_dev * SWEEPS :, :] = jnp.where(
        first_core, diff_ref[tile_rows - EDGE :, :], diff_ref[:EDGE, :]
    )


def adjoint_of(tm, count, coords, misfit_rows, footprints, diffusivity, time_dev):
    slots = footprints.shape[0]
    tile_rows, width = diffusivity.shape
    devices, quarter, wide = misfit_rows.shape
    edge = time_dev * SWEEPS
    vmem = pl.BlockSpec(memory_space=pltpu.VMEM)
    smem = pl.BlockSpec(memory_space=pltpu.SMEM)
    return pl.pallas_call(
        adjoint_kernel,
        out_shape=(
            jax.ShapeDtypeStruct((time_dev * tile_rows, width), bf16),
            jax.ShapeDtypeStruct((edge + EDGE, width), f32),
            jax.ShapeDtypeStruct((edge, width), f32),
        ),
        in_specs=[smem, smem, vmem, vmem, vmem, vmem],
        out_specs=(vmem, vmem, vmem),
        scratch_shapes=[
            pltpu.VMEM((slots, LANES), f32),
            pltpu.VMEM((slots, 2 * LANES), bf16),
            pltpu.VMEM((devices * quarter, wide), bf16),
        ],
        compiler_params=pltpu.CompilerParams(vmem_limit_bytes=12 * MIB),
        name="adjoint",
    )(tm, count, coords, misfit_rows, footprints, diffusivity)


def spread_cov(cov, row_time, col_time, per):
    times = cov.shape[0]
    rows, cols = row_time.shape[0], col_time.shape[1]
    tall = onehot(row_time == iota((rows, times), 1)).astype(f32)
    broad = onehot(col_time == iota((times, cols), 0)).astype(f32)
    highest = lax.Precision.HIGHEST
    wide = dot(dot(tall, cov, highest), broad, highest)
    same = iota((rows, cols), 0) % per == iota((rows, cols), 1) % per
    return jnp.concatenate(split2(jnp.where(same, wide, 0.0)), axis=0)


def mix_kernel(tm_ref, cov_ref, *refs):
    mains, halos, received_ref, (own_ref, twin_ref) = refs[:4], refs[4:8], refs[8], refs[9:]
    time_dev, ext_rows, width = own_ref.shape
    tile_rows = ext_rows - EDGE
    times = cov_ref.shape[0]
    depth, core = tm_ref[0] // 2, tm_ref[0] % 2

    def target_time(per):
        row = iota((2 * time_dev * per, times), 0)
        core_of = jnp.where(row < time_dev * per, core, 1 - core)
        return (2 * depth + core_of) * time_dev + row % (time_dev * per) // per

    def depth_of(col, block):
        return (depth + 4 - col // block) % 4

    def put(full, at, count):
        half = full.shape[0] // 2
        full = full[:half] + full[half:]
        for t in range(time_dev):
            row = t * count
            own_ref[t, at : at + count, :] = full[row : row + count]
            row += time_dev * count
            twin_ref[t, at : at + count, :] = full[row : row + count]

    block = EDGE * time_dev
    col = iota((times, 4 * block), 1)
    source = (2 * depth_of(col, block) + core) * time_dev + col % block // EDGE
    wide = spread_cov(cov_ref[...], target_time(EDGE), source, EDGE)
    for r in range(0, tile_rows, EDGE):
        pieces = [
            main[u * tile_rows + r : u * tile_rows + r + EDGE, :].astype(f32)
            for main in mains
            for u in range(time_dev)
        ]
        put(dot(wide, jnp.concatenate(pieces, axis=0).astype(bf16)), r, EDGE)

    half = SWEEPS * time_dev
    col = iota((times, 8 * half), 1)
    core_of = jnp.where(col % (2 * half) < half, 1 - core, core)
    source = (2 * depth_of(col, 2 * half) + core_of) * time_dev + col % half // SWEEPS
    wide = spread_cov(cov_ref[...], target_time(SWEEPS), source, SWEEPS)
    edges = jnp.concatenate([halo[...] for halo in halos], axis=0)
    put(dot(wide, edges), tile_rows, SWEEPS)
    for t in range(time_dev):
        n = 2 * half + (t % 2) * SWEEPS
        for ref in (own_ref, twin_ref):
            ref[t, tile_rows + SWEEPS :, :] = received_ref[n : n + SWEEPS, :]


def mix(tm, cov, mains, halos, received, shape):
    vmem = pl.BlockSpec(memory_space=pltpu.VMEM)
    whole = jax.ShapeDtypeStruct((shape[0], shape[1] + EDGE, shape[2]), f32)
    return pl.pallas_call(
        mix_kernel,
        out_shape=(whole, whole),
        in_specs=[pl.BlockSpec(memory_space=pltpu.SMEM)] + [vmem] * 10,
        out_specs=(vmem, vmem),
        compiler_params=pltpu.CompilerParams(vmem_limit_bytes=8 * MIB),
        name="mix",
    )(tm, cov, *mains, *halos, received)


def diffuse_kernel(tm_ref, own_ref, twin_ref, diff_ref, out_ref, field, other):
    time_dev, tile_rows, width = out_ref.shape
    ext_rows = field.shape[1]
    first, last = 2 * EDGE, 2 * EDGE + tile_rows
    first_core = tm_ref[0] % 2 == 0
    lower = tile_rows + SWEEPS

    def halo_of(ref):
        return jnp.concatenate([ref[0, lower:, :], ref[1, lower:, :]], axis=0)

    def ordered(a, b):
        return jnp.where(first_core, a, b), jnp.where(first_core, b, a)

    before, after = ordered(halo_of(own_ref), halo_of(twin_ref))
    diff = jnp.concatenate([before, diff_ref[...], after], axis=0)
    column_of = iota(diff.shape, 1)
    here = slice(EDGE, ext_rows - EDGE)
    for buffer in (field, other):
        for t in range(time_dev):
            buffer[t, :first, :] = jnp.zeros((first, width), f32)
            buffer[t, last:, :] = jnp.zeros((ext_rows - last, width), f32)
    for t in range(time_dev):
        field[t, first:last, :] = own_ref[t, :tile_rows, :] + twin_ref[t, :tile_rows, :]
        above, below = ordered(own_ref[t, tile_rows:lower, :], twin_ref[t, tile_rows:lower, :])
        field[t, first - SWEEPS : first, :] = above
        field[t, last : last + SWEEPS, :] = below
    source, target = field, other
    for sweep in range(SWEEPS):
        for t in range(time_dev):
            centre = source[t, here, :]
            left = jnp.where(column_of == 0, 0.0, pltpu.roll(centre, 1, 1))
            right = jnp.where(column_of == width - 1, 0.0, pltpu.roll(centre, width - 1, 1))
            above = source[t, EDGE - 1 : ext_rows - EDGE - 1, :]
            below = source[t, EDGE + 1 : ext_rows - EDGE + 1, :]
            moved = centre + diff * (below + above + right + left - 4.0 * centre)
            if sweep + 1 < SWEEPS:
                target[t, here, :] = moved
            else:
                out_ref[t] = moved[EDGE : EDGE + tile_rows]
        source, target = target, source


def diffuse(tm, own, twin, diffusivity):
    time_dev = own.shape[0]
    tile_rows, width = diffusivity.shape
    field = pltpu.VMEM((time_dev, tile_rows + 4 * EDGE, width), f32)
    vmem = pl.BlockSpec(memory_space=pltpu.VMEM)
    return pl.pallas_call(
        diffuse_kernel,
        out_shape=jax.ShapeDtypeStruct((time_dev, tile_rows, width), f32),
        in_specs=[pl.BlockSpec(memory_space=pltpu.SMEM)] + [vmem] * 3,
        out_specs=vmem,
        scratch_shapes=[field, field],
        compiler_params=pltpu.CompilerParams(vmem_limit_bytes=8 * MIB),
        name="diffuse",
    )(tm, own, twin, diffusivity)


def body(
    fluxes, footprints, block_coords, block_count, observed, obs_weight, time_cov, diffusivity
):
    time_dev, tile_rows, width = fluxes.shape
    n_space, n_tm = lax.axis_size("space"), lax.axis_size("tm")
    devices = n_space * n_tm
    obs_blocks = observed.shape[0] * n_space // LANES
    tm = lax.axis_index("tm").astype(jnp.int32).reshape(1)
    both = ("space", "tm")

    swap = [(i, i ^ 1) for i in range(n_tm)]
    parity = [list(range(n, devices, 2)) for n in range(2)]
    sums, other, kept = forward(
        tm, block_count, block_coords, fluxes, footprints, devices, obs_blocks
    )
    sums = sums + lax.ppermute(other, "tm", swap)
    sums = lax.all_to_all(sums, both, 0, 0, axis_index_groups=parity, tiled=True)
    misfit, halves = misfit_of(tm, sums, obs_weight, observed)
    halves = lax.all_to_all(halves, both, 0, 0, tiled=True)
    main, mine, other = adjoint_of(
        tm, block_count, block_coords, halves, kept, diffusivity, time_dev
    )

    def along(array, steps):
        return lax.ppermute(array, "tm", [(i, (i + 2 * steps) % n_tm) for i in range(n_tm)])

    other = lax.ppermute(other, "tm", swap)
    mains = [main] + [along(main, k) for k in (1, 2, 3)]
    moves = []
    for s in range(n_space - 1):
        for t in range(0, n_tm, 2):
            moves.append((s * n_tm + t, (s + 1) * n_tm + t))
            moves.append(((s + 1) * n_tm + t + 1, s * n_tm + t + 1))
    received = lax.ppermute(jnp.concatenate([other, mine], axis=0), both, moves)
    halo = received[: 2 * time_dev * SWEEPS].astype(bf16)
    halo, mains[3] = lax.optimization_barrier((halo, mains[3]))
    halos = [halo] + [along(halo, k) for k in (1, 2, 3)]
    own, twin = mix(tm, time_cov, mains, halos, received, fluxes.shape)
    twin = lax.ppermute(twin, "tm", swap)
    gradient = diffuse(tm, own, twin, diffusivity)
    return misfit.reshape(-1), gradient


def solution(mesh):
    placed = (
        P("tm", "space", None),
        P(("space", "tm"), None, None),
        P(None, ("space", "tm")),
        P(("space", "tm")),
        P("space"),
        P("space"),
        P(),
        P("space", None),
    )
    return jax.shard_map(
        body,
        mesh=mesh,
        in_specs=placed,
        out_specs=(P(("space", "tm")), P("tm", "space", None)),
        check_vma=False,
    )
```

```python
import functools

import jax
import jax.numpy as jnp
from jax import lax
from jax.experimental import pallas as pl
from jax.experimental.pallas import tpu as pltpu
from jax.sharding import PartitionSpec as P

SWEEPS = 4
LANES = 128
EDGE = 8
MIB = 1024 * 1024

f32 = jnp.float32
bf16 = jnp.bfloat16


def split2(x):
    hi = x.astype(bf16)
    return hi, (x - hi.astype(f32)).astype(bf16)


def iota(shape, dim):
    return lax.broadcasted_iota(jnp.int32, shape, dim)


def onehot(equal):
    return jnp.where(equal, 1.0, 0.0).astype(bf16)


def dot(a, b, precision=None):
    return lax.dot_general(
        a, b, (((1,), (0,)), ((), ())), preferred_element_type=f32, precision=precision
    )


def column(row):
    wide = jnp.broadcast_to(row.astype(f32), (LANES, LANES))
    return jnp.transpose(wide, (1, 0)).astype(jnp.int32)


def forward_kernel(
    tm_ref,
    count_ref,
    coords_hbm,
    flux_hbm,
    foot_ref,
    mine_ref,
    other_ref,
    keep_ref,
    coords_ref,
    flux_ref,
    rhs,
    spread,
    early,
    sems,
    small_sems,
):
    slots = foot_ref.shape[0]
    groups = slots // LANES
    time_dev, tile_rows, width = flux_ref.shape
    across = width // LANES
    steps = time_dev * tile_rows
    bounds = [0] + list(range(LANES // 2, slots, LANES)) + [slots]
    chunks = len(bounds) - 1

    def fetch(k):
        part = pl.ds(bounds[k], bounds[k + 1] - bounds[k])
        return pltpu.make_async_copy(foot_ref.at[part], keep_ref.at[part], sems.at[k])

    small = (
        pltpu.make_async_copy(coords_hbm, coords_ref, small_sems.at[0]),
        pltpu.make_async_copy(flux_hbm, flux_ref, small_sems.at[1]),
    )
    for copy in small:
        copy.start()
    fetch(0).start()
    fetch(1).start()
    for copy in small:
        copy.wait()

    flux = flux_ref[...].reshape(steps, width)
    flux = jnp.concatenate([flux[:, l * LANES : (l + 1) * LANES] for l in range(across)], axis=0)
    lane = iota((LANES, LANES), 1)
    even = (lane & 1) == 0
    for g in range(groups):
        cut = slice(g * LANES, (g + 1) * LANES)
        cell = coords_ref[1:2, cut]
        code = (cell % across) * steps + coords_ref[0:1, cut] * tile_rows + cell // across
        code = column(code)
        pick = jnp.concatenate(
            [onehot(code == lane + j * LANES) for j in range(across * steps // LANES)], axis=1
        )
        piece = jnp.transpose(dot(pick, flux), (1, 0))
        rhs[g, :LANES, :] = jnp.where(even, piece, 0.0).astype(bf16)
        rhs[g, LANES:, :] = jnp.where(even, 0.0, piece).astype(bf16)

    slot = iota((1, slots), 1)
    block = jnp.where(slot < count_ref[0], coords_ref[2:3, :], -1)
    chips, quarter, wide = mine_ref.shape
    cols = wide // LANES
    core = tm_ref[0] % 2

    def summed(n, low, high):
        row = iota((chips * quarter, high - low), 0)
        owner = row // quarter * 2 + (core if n < cols else 1 - core)
        row = (owner * quarter + row % quarter) * cols + n % cols
        full = dot(onehot(row == block[:, low:high]), spread[low:high, :])
        return full[:, :LANES] + full[:, LANES:]

    pair_of_lane = lane // 2
    batch = 8
    total = None
    for k in range(chunks):
        fetch(k).wait()
        if k + 2 < chunks:
            fetch(k + 2).start()
        for b in range(bounds[k], bounds[k + 1], 2 * batch):
            g = b // LANES
            if b % LANES == 0:
                total = jnp.zeros((LANES, LANES), f32)
            blocks = keep_ref[b : b + 2 * batch].reshape(batch, 2, LANES, LANES)
            both = jnp.concatenate([blocks[:, 0], blocks[:, 1]], axis=-1)
            result = dot(both.reshape(batch * LANES, 2 * LANES), rhs[g])
            for j in range(batch):
                p = (b % LANES) // 2 + j
                total = jnp.where(pair_of_lane == p, result[j * LANES : (j + 1) * LANES], total)
            if (b + 2 * batch) % LANES == 0:
                for n, part in enumerate(split2(jnp.transpose(total, (1, 0)))):
                    spread[g * LANES : (g + 1) * LANES, n * LANES : (n + 1) * LANES] = part
                if g == groups - 2:
                    for n in range(2 * cols):
                        early[n] = summed(n, 0, slots - LANES)
    for n in range(2 * cols):
        full = early[n] + summed(n, slots - LANES, slots)
        ref = mine_ref if n < cols else other_ref
        ref[:, :, n % cols * LANES : (n % cols + 1) * LANES] = full.reshape(chips, quarter, LANES)


def forward(tm, count, coords, fluxes, footprints, devices, obs_blocks):
    per = obs_blocks // devices
    slots = footprints.shape[0]
    cols = per // 4
    vmem = pl.BlockSpec(memory_space=pltpu.VMEM)
    smem = pl.BlockSpec(memory_space=pltpu.SMEM)
    hbm = pl.BlockSpec(memory_space=pltpu.HBM)
    return pl.pallas_call(
        forward_kernel,
        out_shape=(
            pltpu.VMEM((devices // 2, 4, cols * LANES), f32),
            pltpu.VMEM((devices // 2, 4, cols * LANES), f32),
            pltpu.VMEM(footprints.shape, bf16),
        ),
        in_specs=[smem, smem, hbm, hbm, hbm],
        out_specs=(vmem, vmem, vmem),
        scratch_shapes=[
            pltpu.VMEM(coords.shape, jnp.int32),
            pltpu.VMEM(fluxes.shape, bf16),
            pltpu.VMEM((slots // LANES, 2 * LANES, LANES), bf16),
            pltpu.VMEM((slots, 2 * LANES), bf16),
            pltpu.VMEM((2 * cols, devices * 2, LANES), f32),
            pltpu.SemaphoreType.DMA((slots // LANES + 1,)),
            pltpu.SemaphoreType.DMA((2,)),
        ],
        compiler_params=pltpu.CompilerParams(vmem_limit_bytes=38 * MIB),
        name="forward",
    )(tm, count, coords, fluxes, footprints)


def misfit_kernel(tm_ref, sums_ref, weight_ref, observed_ref, out_ref, half_ref):
    devices, quarter, wide = sums_ref.shape
    cols = wide // LANES
    total = jnp.sum(sums_ref[...], axis=0)
    base = tm_ref[0] * (quarter * cols)

    def own(ref):
        return jnp.concatenate(
            [ref[pl.ds(base + l, quarter, stride=cols), :] for l in range(cols)], axis=1
        )

    misfit = own(weight_ref) * (total - own(observed_ref))
    for q in range(quarter):
        for l in range(cols):
            out_ref[q * cols + l : q * cols + l + 1, :] = misfit[
                q : q + 1, l * LANES : (l + 1) * LANES
            ]
    half_ref[...] = jnp.broadcast_to(misfit[None], half_ref.shape).astype(bf16)


def misfit_of(tm, sums, weight, observed):
    devices, quarter, wide = sums.shape
    vmem = pl.BlockSpec(memory_space=pltpu.VMEM)
    return pl.pallas_call(
        misfit_kernel,
        out_shape=(
            jax.ShapeDtypeStruct((quarter * wide // LANES, LANES), f32),
            jax.ShapeDtypeStruct((2 * devices, quarter, wide), bf16),
        ),
        in_specs=[pl.BlockSpec(memory_space=pltpu.SMEM), vmem, vmem, vmem],
        out_specs=(vmem, vmem),
        compiler_params=pltpu.CompilerParams(vmem_limit_bytes=4 * MIB),
        name="misfit",
    )(tm, sums, weight.reshape(-1, LANES), observed.reshape(-1, LANES))


def adjoint_kernel(
    tm_ref,
    count_ref,
    coords_ref,
    misfit_ref,
    foot_ref,
    diff_ref,
    main_ref,
    mine_ref,
    other_ref,
    contrib,
    spread,
    rows_ref,
):
    slots = foot_ref.shape[0]
    groups = slots // LANES
    devices, quarter, wide = misfit_ref.shape
    cols = wide // LANES
    rows = devices * quarter
    tile_rows = diff_ref.shape[0]
    lane = iota((LANES, LANES), 1)
    rows_ref[...] = misfit_ref[...].astype(f32).reshape(rows, wide).astype(bf16)
    for g in range(groups):
        block = column(coords_ref[2:3, g * LANES : (g + 1) * LANES])
        chosen = jnp.zeros((LANES, LANES), f32)
        for l in range(cols):
            pick = jnp.concatenate(
                [onehot(block == (lane + j * LANES) * cols + l) for j in range(rows // LANES)], axis=1
            )
            chosen = chosen + dot(pick, rows_ref[:, l * LANES : (l + 1) * LANES])
        contrib[g * LANES : (g + 1) * LANES, :] = chosen

    batch = 16
    sub = iota((batch, LANES), 0)
    for at in range(0, slots, batch):
        some = contrib[at : at + batch, :]
        left = jnp.concatenate(
            [jnp.where(sub == j, some, 0.0).astype(bf16) for j in range(batch)], axis=1
        )
        blocks = foot_ref[at : at + batch].reshape(batch * LANES, LANES)
        for n, part in enumerate(split2(dot(left, blocks))):
            spread[at : at + batch, n * LANES : (n + 1) * LANES] = part

    time_dev = main_ref.shape[0] // tile_rows
    width = main_ref.shape[1]
    across = width // LANES
    steps = time_dev * tile_rows
    first_core = tm_ref[0] % 2 == 0
    slot = iota((1, slots), 1)
    cell = coords_ref[1:2, :]
    code = coords_ref[0:1, :] * tile_rows + cell // across
    code = jnp.where(slot < count_ref[0], code, -1)
    for l in range(across):
        cut = slice(l * LANES, (l + 1) * LANES)
        pick = onehot(iota((steps, slots), 0) == jnp.where(cell % across == l, code, -1))
        full = dot(pick, spread[...])
        summed = full[:, :LANES] + full[:, LANES:]
        main_ref[:, cut] = summed.astype(bf16)
        for t in range(time_dev):
            row, at = t * tile_rows, t * SWEEPS
            down = summed[row + tile_rows - SWEEPS : row + tile_rows]
            up = summed[row : row + SWEEPS]
            mine_ref[at : at + SWEEPS, cut] = jnp.where(first_core, down, up)
            other_ref[at : at + SWEEPS, cut] = jnp.where(first_core, up, down)
    mine_ref[time_dev * SWEEPS :, :] = jnp.where(
        first_core, diff_ref[tile_rows - EDGE :, :], diff_ref[:EDGE, :]
    )


def adjoint_of(tm, count, coords, misfit_rows, footprints, diffusivity, time_dev):
    slots = footprints.shape[0]
    tile_rows, width = diffusivity.shape
    devices, quarter, wide = misfit_rows.shape
    edge = time_dev * SWEEPS
    vmem = pl.BlockSpec(memory_space=pltpu.VMEM)
    smem = pl.BlockSpec(memory_space=pltpu.SMEM)
    return pl.pallas_call(
        adjoint_kernel,
        out_shape=(
            jax.ShapeDtypeStruct((time_dev * tile_rows, width), bf16),
            jax.ShapeDtypeStruct((edge + EDGE, width), f32),
            jax.ShapeDtypeStruct((edge, width), f32),
        ),
        in_specs=[smem, smem, vmem, vmem, vmem, vmem],
        out_specs=(vmem, vmem, vmem),
        scratch_shapes=[
            pltpu.VMEM((slots, LANES), f32),
            pltpu.VMEM((slots, 2 * LANES), bf16),
            pltpu.VMEM((devices * quarter, wide), bf16),
        ],
        compiler_params=pltpu.CompilerParams(vmem_limit_bytes=12 * MIB),
        name="adjoint",
    )(tm, count, coords, misfit_rows, footprints, diffusivity)


def spread_cov(cov, row_time, col_time, per):
    times = cov.shape[0]
    rows, cols = row_time.shape[0], col_time.shape[1]
    tall = onehot(row_time == iota((rows, times), 1)).astype(f32)
    broad = onehot(col_time == iota((times, cols), 0)).astype(f32)
    highest = lax.Precision.HIGHEST
    wide = dot(dot(tall, cov, highest), broad, highest)
    same = iota((rows, cols), 0) % per == iota((rows, cols), 1) % per
    return jnp.concatenate(split2(jnp.where(same, wide, 0.0)), axis=0)


def weights_kernel(tm_ref, cov_ref, main_ref, halo_ref):
    times = cov_ref.shape[0]
    time_dev = main_ref.shape[2] // (4 * EDGE)
    depth, core = tm_ref[0] // 2, tm_ref[0] % 2

    def target_time(per, n):
        row = iota((time_dev * per, times), 0)
        return (2 * depth + (core if n == 0 else 1 - core)) * time_dev + row // per

    def depth_of(col, block):
        return (depth + 4 - col // block) % 4

    block = EDGE * time_dev
    col = iota((times, 4 * block), 1)
    source = (2 * depth_of(col, block) + core) * time_dev + col % block // EDGE
    half = SWEEPS * time_dev
    col = iota((times, 8 * half), 1)
    core_of = jnp.where(col % (2 * half) < half, 1 - core, core)
    edge_source = (2 * depth_of(col, 2 * half) + core_of) * time_dev + col % half // SWEEPS
    for n in range(2):
        main_ref[n] = spread_cov(cov_ref[...], target_time(EDGE, n), source, EDGE)
        halo_ref[n] = spread_cov(cov_ref[...], target_time(SWEEPS, n), edge_source, SWEEPS)


def weights(tm, cov, time_dev):
    vmem = pl.BlockSpec(memory_space=pltpu.VMEM)
    block = time_dev * EDGE
    half = time_dev * SWEEPS
    return pl.pallas_call(
        weights_kernel,
        out_shape=(
            jax.ShapeDtypeStruct((2, 2 * block, 4 * block), bf16),
            jax.ShapeDtypeStruct((2, 2 * half, 8 * half), bf16),
        ),
        in_specs=[pl.BlockSpec(memory_space=pltpu.SMEM), vmem],
        out_specs=(vmem, vmem),
        compiler_params=pltpu.CompilerParams(vmem_limit_bytes=2 * MIB),
        name="weights",
    )(tm, cov)


def mix_kernel(twin, main_weight_ref, halo_weight_ref, *refs):
    mains, halos, received_ref, out_ref = refs[:4], refs[4:8], refs[8], refs[9]
    time_dev, ext_rows, width = out_ref.shape
    tile_rows = ext_rows - EDGE

    def put(full, at, count):
        half = full.shape[0] // 2
        full = full[:half] + full[half:]
        for t in range(time_dev):
            out_ref[t, at : at + count, :] = full[t * count : (t + 1) * count]

    wide = main_weight_ref[int(twin)]
    for r in range(0, tile_rows, EDGE):
        pieces = [
            main[u * tile_rows + r : u * tile_rows + r + EDGE, :].astype(f32)
            for main in mains
            for u in range(time_dev)
        ]
        put(dot(wide, jnp.concatenate(pieces, axis=0).astype(bf16)), r, EDGE)
    edges = jnp.concatenate([halo[...] for halo in halos], axis=0)
    put(dot(halo_weight_ref[int(twin)], edges), tile_rows, SWEEPS)
    base = 2 * time_dev * SWEEPS
    for t in range(time_dev):
        n = base + (t % 2) * SWEEPS
        out_ref[t, tile_rows + SWEEPS :, :] = received_ref[n : n + SWEEPS, :]


def mix(twin, wide, mains, halos, received, shape):
    vmem = pl.BlockSpec(memory_space=pltpu.VMEM)
    return pl.pallas_call(
        functools.partial(mix_kernel, twin),
        out_shape=jax.ShapeDtypeStruct((shape[0], shape[1] + EDGE, shape[2]), f32),
        in_specs=[vmem] * 11,
        out_specs=vmem,
        compiler_params=pltpu.CompilerParams(vmem_limit_bytes=8 * MIB),
        name="mix_twin" if twin else "mix_own",
    )(*wide, *mains, *halos, received)


def diffuse_kernel(tm_ref, own_ref, twin_ref, diff_ref, out_ref, field, other, staged, sems):
    time_dev, tile_rows, width = staged.shape
    ext_rows = field.shape[1]
    first, last = 2 * EDGE, 2 * EDGE + tile_rows
    first_core = tm_ref[0] % 2 == 0
    lower = tile_rows + SWEEPS

    def halo_of(ref):
        return jnp.concatenate([ref[0, lower:, :], ref[1, lower:, :]], axis=0)

    def ordered(a, b):
        return jnp.where(first_core, a, b), jnp.where(first_core, b, a)

    def leave(t):
        return pltpu.make_async_copy(staged.at[t], out_ref.at[t], sems.at[t])

    before, after = ordered(halo_of(own_ref), halo_of(twin_ref))
    diff = jnp.concatenate([before, diff_ref[...], after], axis=0)
    keep = 1.0 - 4.0 * diff
    column_of = iota(diff.shape, 1)
    here = slice(EDGE, ext_rows - EDGE)
    for buffer in (field, other):
        for t in range(time_dev):
            buffer[t, :first, :] = jnp.zeros((first, width), f32)
            buffer[t, last:, :] = jnp.zeros((ext_rows - last, width), f32)
    for t in range(time_dev):
        field[t, first:last, :] = own_ref[t, :tile_rows, :] + twin_ref[t, :tile_rows, :]
        above, below = ordered(own_ref[t, tile_rows:lower, :], twin_ref[t, tile_rows:lower, :])
        field[t, first - SWEEPS : first, :] = above
        field[t, last : last + SWEEPS, :] = below
    source, target = field, other
    for sweep in range(SWEEPS):
        for t in range(time_dev):
            centre = source[t, here, :]
            left = jnp.where(column_of == 0, 0.0, pltpu.roll(centre, 1, 1))
            right = jnp.where(column_of == width - 1, 0.0, pltpu.roll(centre, width - 1, 1))
            above = source[t, EDGE - 1 : ext_rows - EDGE - 1, :]
            below = source[t, EDGE + 1 : ext_rows - EDGE + 1, :]
            moved = keep * centre + diff * (below + above + right + left)
            if sweep + 1 < SWEEPS:
                target[t, here, :] = moved
            else:
                staged[t] = moved[EDGE : EDGE + tile_rows]
                leave(t).start()
        source, target = target, source
    for t in range(time_dev):
        leave(t).wait()


def diffuse(tm, own, twin, diffusivity):
    time_dev = own.shape[0]
    tile_rows, width = diffusivity.shape
    field = pltpu.VMEM((time_dev, tile_rows + 4 * EDGE, width), f32)
    vmem = pl.BlockSpec(memory_space=pltpu.VMEM)
    shape = (time_dev, tile_rows, width)
    return pl.pallas_call(
        diffuse_kernel,
        out_shape=jax.ShapeDtypeStruct(shape, f32),
        in_specs=[pl.BlockSpec(memory_space=pltpu.SMEM)] + [vmem] * 3,
        out_specs=pl.BlockSpec(memory_space=pltpu.HBM),
        scratch_shapes=[field, field, pltpu.VMEM(shape, f32), pltpu.SemaphoreType.DMA((time_dev,))],
        compiler_params=pltpu.CompilerParams(vmem_limit_bytes=10 * MIB),
        name="diffuse",
    )(tm, own, twin, diffusivity)


def body(
    fluxes, footprints, block_coords, block_count, observed, obs_weight, time_cov, diffusivity
):
    time_dev, tile_rows, width = fluxes.shape
    n_space, n_tm = lax.axis_size("space"), lax.axis_size("tm")
    devices = n_space * n_tm
    obs_blocks = observed.shape[0] * n_space // LANES
    tm = lax.axis_index("tm").astype(jnp.int32).reshape(1)
    both = ("space", "tm")

    swap = [(i, i ^ 1) for i in range(n_tm)]
    parity = [list(range(n, devices, 2)) for n in range(2)]
    sums, other, kept = forward(
        tm, block_count, block_coords, fluxes, footprints, devices, obs_blocks
    )
    sums = sums + lax.ppermute(other, "tm", swap)
    sums = lax.all_to_all(sums, both, 0, 0, axis_index_groups=parity, tiled=True)
    misfit, halves = misfit_of(tm, sums, obs_weight, observed)
    halves = lax.all_to_all(halves, both, 0, 0, tiled=True)
    main, mine, other = adjoint_of(
        tm, block_count, block_coords, halves, kept, diffusivity, time_dev
    )

    def along(array, steps):
        return lax.ppermute(array, "tm", [(i, (i + 2 * steps) % n_tm) for i in range(n_tm)])

    other = lax.ppermute(other, "tm", swap)
    mains = [main] + [along(main, k) for k in (1, 2, 3)]
    moves = []
    for s in range(n_space - 1):
        for t in range(0, n_tm, 2):
            moves.append((s * n_tm + t, (s + 1) * n_tm + t))
            moves.append(((s + 1) * n_tm + t + 1, s * n_tm + t + 1))
    payload, cov = lax.optimization_barrier((jnp.concatenate([other, mine], axis=0), time_cov))
    received = lax.ppermute(payload, both, moves)
    wide = weights(tm, cov, time_dev)
    halo = received[: 2 * time_dev * SWEEPS].astype(bf16)
    halo, mains[3] = lax.optimization_barrier((halo, mains[3]))
    halos = [halo] + [along(halo, k) for k in (1, 2, 3)]
    held = (wide, mains, halos, received, fluxes.shape)
    twin = lax.ppermute(mix(True, *held), "tm", swap)
    own = mix(False, *held)
    gradient = diffuse(tm, own, twin, diffusivity)
    return misfit.reshape(-1), gradient


def solution(mesh):
    placed = (
        P("tm", "space", None),
        P(("space", "tm"), None, None),
        P(None, ("space", "tm")),
        P(("space", "tm")),
        P("space"),
        P("space"),
        P(),
        P("space", None),
    )
    return jax.shard_map(
        body,
        mesh=mesh,
        in_specs=placed,
        out_specs=(P(("space", "tm")), P("tm", "space", None)),
        check_vma=False,
    )
```

```python
import functools

import jax
import jax.numpy as jnp
from jax import lax
from jax.experimental import pallas as pl
from jax.experimental.pallas import tpu as pltpu
from jax.sharding import PartitionSpec as P

SWEEPS = 4
LANES = 128
EDGE = 8
MIB = 1024 * 1024

f32 = jnp.float32
bf16 = jnp.bfloat16


def split2(x):
    hi = x.astype(bf16)
    return hi, (x - hi.astype(f32)).astype(bf16)


def iota(shape, dim):
    return lax.broadcasted_iota(jnp.int32, shape, dim)


def onehot(equal):
    return jnp.where(equal, 1.0, 0.0).astype(bf16)


def dot(a, b, precision=None):
    return lax.dot_general(
        a, b, (((1,), (0,)), ((), ())), preferred_element_type=f32, precision=precision
    )


def column(row):
    wide = jnp.broadcast_to(row.astype(f32), (LANES, LANES))
    return jnp.transpose(wide, (1, 0)).astype(jnp.int32)


def forward_kernel(
    tm_ref,
    count_ref,
    coords_hbm,
    flux_hbm,
    foot_ref,
    mine_ref,
    other_ref,
    keep_ref,
    coords_ref,
    flux_ref,
    rhs,
    spread,
    early,
    sems,
    small_sems,
):
    slots = foot_ref.shape[0]
    groups = slots // LANES
    time_dev, tile_rows, width = flux_ref.shape
    across = width // LANES
    steps = time_dev * tile_rows
    bounds = [0] + list(range(LANES // 2, slots, LANES)) + [slots]
    chunks = len(bounds) - 1

    def fetch(k):
        part = pl.ds(bounds[k], bounds[k + 1] - bounds[k])
        return pltpu.make_async_copy(foot_ref.at[part], keep_ref.at[part], sems.at[k])

    small = (
        pltpu.make_async_copy(coords_hbm, coords_ref, small_sems.at[0]),
        pltpu.make_async_copy(flux_hbm, flux_ref, small_sems.at[1]),
    )
    for copy in small:
        copy.start()
    fetch(0).start()
    fetch(1).start()
    for copy in small:
        copy.wait()

    flux = flux_ref[...].reshape(steps, width)
    flux = jnp.concatenate([flux[:, l * LANES : (l + 1) * LANES] for l in range(across)], axis=0)
    lane = iota((LANES, LANES), 1)
    even = (lane & 1) == 0
    for g in range(groups):
        cut = slice(g * LANES, (g + 1) * LANES)
        cell = coords_ref[1:2, cut]
        code = (cell % across) * steps + coords_ref[0:1, cut] * tile_rows + cell // across
        code = column(code)
        pick = jnp.concatenate(
            [onehot(code == lane + j * LANES) for j in range(across * steps // LANES)], axis=1
        )
        piece = jnp.transpose(dot(pick, flux), (1, 0))
        rhs[g, :LANES, :] = jnp.where(even, piece, 0.0).astype(bf16)
        rhs[g, LANES:, :] = jnp.where(even, 0.0, piece).astype(bf16)

    slot = iota((1, slots), 1)
    block = jnp.where(slot < count_ref[0], coords_ref[2:3, :], -1)
    chips, quarter, wide = mine_ref.shape
    cols = wide // LANES
    core = tm_ref[0] % 2

    def summed(n, low, high):
        row = iota((chips * quarter, high - low), 0)
        owner = row // quarter * 2 + (core if n < cols else 1 - core)
        row = (owner * quarter + row % quarter) * cols + n % cols
        full = dot(onehot(row == block[:, low:high]), spread[low:high, :])
        return full[:, :LANES] + full[:, LANES:]

    pair_of_lane = lane // 2
    batch = 8
    total = None
    for k in range(chunks):
        fetch(k).wait()
        if k + 2 < chunks:
            fetch(k + 2).start()
        for b in range(bounds[k], bounds[k + 1], 2 * batch):
            g = b // LANES
            if b % LANES == 0:
                total = jnp.zeros((LANES, LANES), f32)
            blocks = keep_ref[b : b + 2 * batch].reshape(batch, 2, LANES, LANES)
            both = jnp.concatenate([blocks[:, 0], blocks[:, 1]], axis=-1)
            result = dot(both.reshape(batch * LANES, 2 * LANES), rhs[g])
            for j in range(batch):
                p = (b % LANES) // 2 + j
                total = jnp.where(pair_of_lane == p, result[j * LANES : (j + 1) * LANES], total)
            if (b + 2 * batch) % LANES == 0:
                for n, part in enumerate(split2(jnp.transpose(total, (1, 0)))):
                    spread[g * LANES : (g + 1) * LANES, n * LANES : (n + 1) * LANES] = part
                if g == groups - 2:
                    for n in range(2 * cols):
                        early[n] = summed(n, 0, slots - LANES)
    for n in range(2 * cols):
        full = early[n] + summed(n, slots - LANES, slots)
        ref = mine_ref if n < cols else other_ref
        ref[:, :, n % cols * LANES : (n % cols + 1) * LANES] = full.reshape(chips, quarter, LANES)


def forward(tm, count, coords, fluxes, footprints, devices, obs_blocks):
    per = obs_blocks // devices
    slots = footprints.shape[0]
    cols = per // 4
    vmem = pl.BlockSpec(memory_space=pltpu.VMEM)
    smem = pl.BlockSpec(memory_space=pltpu.SMEM)
    hbm = pl.BlockSpec(memory_space=pltpu.HBM)
    return pl.pallas_call(
        forward_kernel,
        out_shape=(
            pltpu.VMEM((devices // 2, 4, cols * LANES), f32),
            pltpu.VMEM((devices // 2, 4, cols * LANES), f32),
            pltpu.VMEM(footprints.shape, bf16),
        ),
        in_specs=[smem, smem, hbm, hbm, hbm],
        out_specs=(vmem, vmem, vmem),
        scratch_shapes=[
            pltpu.VMEM(coords.shape, jnp.int32),
            pltpu.VMEM(fluxes.shape, bf16),
            pltpu.VMEM((slots // LANES, 2 * LANES, LANES), bf16),
            pltpu.VMEM((slots, 2 * LANES), bf16),
            pltpu.VMEM((2 * cols, devices * 2, LANES), f32),
            pltpu.SemaphoreType.DMA((slots // LANES + 1,)),
            pltpu.SemaphoreType.DMA((2,)),
        ],
        compiler_params=pltpu.CompilerParams(vmem_limit_bytes=38 * MIB),
        name="forward",
    )(tm, count, coords, fluxes, footprints)


def misfit_kernel(tm_ref, sums_ref, weight_ref, observed_ref, out_ref, half_ref):
    devices, quarter, wide = sums_ref.shape
    cols = wide // LANES
    total = jnp.sum(sums_ref[...], axis=0)
    base = tm_ref[0] * (quarter * cols)

    def own(ref):
        block = ref[pl.ds(base, quarter * cols), :]
        return jnp.concatenate(
            [
                jnp.concatenate(
                    [block[q * cols + l : q * cols + l + 1] for q in range(quarter)], axis=0
                )
                for l in range(cols)
            ],
            axis=1,
        )

    misfit = own(weight_ref) * (total - own(observed_ref))
    for q in range(quarter):
        for l in range(cols):
            out_ref[q * cols + l : q * cols + l + 1, :] = misfit[
                q : q + 1, l * LANES : (l + 1) * LANES
            ]
    half_ref[...] = jnp.broadcast_to(misfit[None], half_ref.shape).astype(bf16)


def misfit_of(tm, sums, weight, observed):
    devices, quarter, wide = sums.shape
    vmem = pl.BlockSpec(memory_space=pltpu.VMEM)
    return pl.pallas_call(
        misfit_kernel,
        out_shape=(
            jax.ShapeDtypeStruct((quarter * wide // LANES, LANES), f32),
            jax.ShapeDtypeStruct((2 * devices, quarter, wide), bf16),
        ),
        in_specs=[pl.BlockSpec(memory_space=pltpu.SMEM), vmem, vmem, vmem],
        out_specs=(vmem, vmem),
        compiler_params=pltpu.CompilerParams(vmem_limit_bytes=4 * MIB),
        name="misfit",
    )(tm, sums, weight.reshape(-1, LANES), observed.reshape(-1, LANES))


def adjoint_kernel(
    tm_ref,
    count_ref,
    coords_ref,
    misfit_ref,
    foot_ref,
    diff_ref,
    main_ref,
    mine_ref,
    other_ref,
    contrib,
    spread,
    rows_ref,
):
    slots = foot_ref.shape[0]
    groups = slots // LANES
    devices, quarter, wide = misfit_ref.shape
    cols = wide // LANES
    rows = devices * quarter
    tile_rows = diff_ref.shape[0]
    lane = iota((LANES, LANES), 1)
    rows_ref[...] = misfit_ref[...].astype(f32).reshape(rows, wide).astype(bf16)
    for g in range(groups):
        block = column(coords_ref[2:3, g * LANES : (g + 1) * LANES])
        chosen = jnp.zeros((LANES, LANES), f32)
        for l in range(cols):
            pick = jnp.concatenate(
                [onehot(block == (lane + j * LANES) * cols + l) for j in range(rows // LANES)], axis=1
            )
            chosen = chosen + dot(pick, rows_ref[:, l * LANES : (l + 1) * LANES])
        contrib[g * LANES : (g + 1) * LANES, :] = chosen

    batch = 16
    sub = iota((batch, LANES), 0)
    for at in range(0, slots, batch):
        some = contrib[at : at + batch, :]
        left = jnp.concatenate(
            [jnp.where(sub == j, some, 0.0).astype(bf16) for j in range(batch)], axis=1
        )
        blocks = foot_ref[at : at + batch].reshape(batch * LANES, LANES)
        for n, part in enumerate(split2(dot(left, blocks))):
            spread[at : at + batch, n * LANES : (n + 1) * LANES] = part

    time_dev = main_ref.shape[0] // tile_rows
    width = main_ref.shape[1]
    across = width // LANES
    steps = time_dev * tile_rows
    first_core = tm_ref[0] % 2 == 0
    slot = iota((1, slots), 1)
    cell = coords_ref[1:2, :]
    code = coords_ref[0:1, :] * tile_rows + cell // across
    code = jnp.where(slot < count_ref[0], code, -1)
    for l in range(across):
        cut = slice(l * LANES, (l + 1) * LANES)
        pick = onehot(iota((steps, slots), 0) == jnp.where(cell % across == l, code, -1))
        full = dot(pick, spread[...])
        summed = full[:, :LANES] + full[:, LANES:]
        main_ref[:, cut] = summed.astype(bf16)
        for t in range(time_dev):
            row, at = t * tile_rows, t * SWEEPS
            down = summed[row + tile_rows - SWEEPS : row + tile_rows]
            up = summed[row : row + SWEEPS]
            mine_ref[at : at + SWEEPS, cut] = jnp.where(first_core, down, up)
            other_ref[at : at + SWEEPS, cut] = jnp.where(first_core, up, down)
    mine_ref[time_dev * SWEEPS :, :] = jnp.where(
        first_core, diff_ref[tile_rows - EDGE :, :], diff_ref[:EDGE, :]
    )


def adjoint_of(tm, count, coords, misfit_rows, footprints, diffusivity, time_dev):
    slots = footprints.shape[0]
    tile_rows, width = diffusivity.shape
    devices, quarter, wide = misfit_rows.shape
    edge = time_dev * SWEEPS
    vmem = pl.BlockSpec(memory_space=pltpu.VMEM)
    smem = pl.BlockSpec(memory_space=pltpu.SMEM)
    return pl.pallas_call(
        adjoint_kernel,
        out_shape=(
            jax.ShapeDtypeStruct((time_dev * tile_rows, width), bf16),
            jax.ShapeDtypeStruct((edge + EDGE, width), f32),
            jax.ShapeDtypeStruct((edge, width), f32),
        ),
        in_specs=[smem, smem, vmem, vmem, vmem, vmem],
        out_specs=(vmem, vmem, vmem),
        scratch_shapes=[
            pltpu.VMEM((slots, LANES), f32),
            pltpu.VMEM((slots, 2 * LANES), bf16),
            pltpu.VMEM((devices * quarter, wide), bf16),
        ],
        compiler_params=pltpu.CompilerParams(vmem_limit_bytes=12 * MIB),
        name="adjoint",
    )(tm, count, coords, misfit_rows, footprints, diffusivity)


def spread_cov(cov, row_time, col_time, per):
    times = cov.shape[0]
    rows, cols = row_time.shape[0], col_time.shape[1]
    tall = onehot(row_time == iota((rows, times), 1)).astype(f32)
    broad = onehot(col_time == iota((times, cols), 0)).astype(f32)
    highest = lax.Precision.HIGHEST
    wide = dot(dot(tall, cov, highest), broad, highest)
    same = iota((rows, cols), 0) % per == iota((rows, cols), 1) % per
    return jnp.concatenate(split2(jnp.where(same, wide, 0.0)), axis=0)


def weights_kernel(tm_ref, cov_ref, main_ref, halo_ref):
    times = cov_ref.shape[0]
    time_dev = main_ref.shape[2] // (4 * EDGE)
    depth, core = tm_ref[0] // 2, tm_ref[0] % 2

    def target_time(per, n):
        row = iota((time_dev * per, times), 0)
        return (2 * depth + (core if n == 0 else 1 - core)) * time_dev + row // per

    def depth_of(col, block):
        return (depth + 4 - col // block) % 4

    block = EDGE * time_dev
    col = iota((times, 4 * block), 1)
    source = (2 * depth_of(col, block) + core) * time_dev + col % block // EDGE
    half = SWEEPS * time_dev
    col = iota((times, 8 * half), 1)
    core_of = jnp.where(col % (2 * half) < half, 1 - core, core)
    edge_source = (2 * depth_of(col, 2 * half) + core_of) * time_dev + col % half // SWEEPS
    for n in range(2):
        main_ref[n] = spread_cov(cov_ref[...], target_time(EDGE, n), source, EDGE)
        halo_ref[n] = spread_cov(cov_ref[...], target_time(SWEEPS, n), edge_source, SWEEPS)


def weights(tm, cov, time_dev):
    vmem = pl.BlockSpec(memory_space=pltpu.VMEM)
    block = time_dev * EDGE
    half = time_dev * SWEEPS
    return pl.pallas_call(
        weights_kernel,
        out_shape=(
            jax.ShapeDtypeStruct((2, 2 * block, 4 * block), bf16),
            jax.ShapeDtypeStruct((2, 2 * half, 8 * half), bf16),
        ),
        in_specs=[pl.BlockSpec(memory_space=pltpu.SMEM), vmem],
        out_specs=(vmem, vmem),
        compiler_params=pltpu.CompilerParams(vmem_limit_bytes=2 * MIB),
        name="weights",
    )(tm, cov)


def mix_kernel(twin, main_weight_ref, halo_weight_ref, *refs):
    mains, halos, received_ref, out_ref = refs[:4], refs[4:8], refs[8], refs[9]
    time_dev, ext_rows, width = out_ref.shape
    tile_rows = ext_rows - EDGE

    def put(full, at, count):
        half = full.shape[0] // 2
        full = full[:half] + full[half:]
        for t in range(time_dev):
            out_ref[t, at : at + count, :] = full[t * count : (t + 1) * count]

    wide = main_weight_ref[int(twin)]
    for r in range(0, tile_rows, EDGE):
        pieces = [
            main[u * tile_rows + r : u * tile_rows + r + EDGE, :].astype(f32)
            for main in mains
            for u in range(time_dev)
        ]
        put(dot(wide, jnp.concatenate(pieces, axis=0).astype(bf16)), r, EDGE)
    edges = jnp.concatenate([halo[...] for halo in halos], axis=0)
    put(dot(halo_weight_ref[int(twin)], edges), tile_rows, SWEEPS)
    base = 2 * time_dev * SWEEPS
    for t in range(time_dev):
        n = base + (t % 2) * SWEEPS
        out_ref[t, tile_rows + SWEEPS :, :] = received_ref[n : n + SWEEPS, :]


def mix(twin, wide, mains, halos, received, shape):
    vmem = pl.BlockSpec(memory_space=pltpu.VMEM)
    return pl.pallas_call(
        functools.partial(mix_kernel, twin),
        out_shape=jax.ShapeDtypeStruct((shape[0], shape[1] + EDGE, shape[2]), f32),
        in_specs=[vmem] * 11,
        out_specs=vmem,
        compiler_params=pltpu.CompilerParams(vmem_limit_bytes=8 * MIB),
        name="mix_twin" if twin else "mix_own",
    )(*wide, *mains, *halos, received)


def diffuse_kernel(tm_ref, own_ref, twin_ref, diff_ref, out_ref, field, other, staged, sems):
    time_dev, tile_rows, width = staged.shape
    ext_rows = field.shape[1]
    first, last = 2 * EDGE, 2 * EDGE + tile_rows
    first_core = tm_ref[0] % 2 == 0
    lower = tile_rows + SWEEPS

    def halo_of(ref):
        return jnp.concatenate([ref[0, lower:, :], ref[1, lower:, :]], axis=0)

    def ordered(a, b):
        return jnp.where(first_core, a, b), jnp.where(first_core, b, a)

    def leave(t):
        return pltpu.make_async_copy(staged.at[t], out_ref.at[t], sems.at[t])

    before, after = ordered(halo_of(own_ref), halo_of(twin_ref))
    diff = jnp.concatenate([before, diff_ref[...], after], axis=0)
    keep = 1.0 - 4.0 * diff
    column_of = iota(diff.shape, 1)
    here = slice(EDGE, ext_rows - EDGE)
    for buffer in (field, other):
        for t in range(time_dev):
            buffer[t, :first, :] = jnp.zeros((first, width), f32)
            buffer[t, last:, :] = jnp.zeros((ext_rows - last, width), f32)
    for t in range(time_dev):
        field[t, first:last, :] = own_ref[t, :tile_rows, :] + twin_ref[t, :tile_rows, :]
        above, below = ordered(own_ref[t, tile_rows:lower, :], twin_ref[t, tile_rows:lower, :])
        field[t, first - SWEEPS : first, :] = above
        field[t, last : last + SWEEPS, :] = below
    source, target = field, other
    for sweep in range(SWEEPS):
        for t in range(time_dev):
            centre = source[t, here, :]
            left = jnp.where(column_of == 0, 0.0, pltpu.roll(centre, 1, 1))
            right = jnp.where(column_of == width - 1, 0.0, pltpu.roll(centre, width - 1, 1))
            above = source[t, EDGE - 1 : ext_rows - EDGE - 1, :]
            below = source[t, EDGE + 1 : ext_rows - EDGE + 1, :]
            moved = keep * centre + diff * (below + above + right + left)
            if sweep + 1 < SWEEPS:
                target[t, here, :] = moved
            else:
                staged[t] = moved[EDGE : EDGE + tile_rows]
                leave(t).start()
        source, target = target, source
    for t in range(time_dev):
        leave(t).wait()


def diffuse(tm, own, twin, diffusivity):
    time_dev = own.shape[0]
    tile_rows, width = diffusivity.shape
    field = pltpu.VMEM((time_dev, tile_rows + 4 * EDGE, width), f32)
    vmem = pl.BlockSpec(memory_space=pltpu.VMEM)
    shape = (time_dev, tile_rows, width)
    return pl.pallas_call(
        diffuse_kernel,
        out_shape=jax.ShapeDtypeStruct(shape, f32),
        in_specs=[pl.BlockSpec(memory_space=pltpu.SMEM)] + [vmem] * 3,
        out_specs=pl.BlockSpec(memory_space=pltpu.HBM),
        scratch_shapes=[field, field, pltpu.VMEM(shape, f32), pltpu.SemaphoreType.DMA((time_dev,))],
        compiler_params=pltpu.CompilerParams(vmem_limit_bytes=10 * MIB),
        name="diffuse",
    )(tm, own, twin, diffusivity)


def body(
    fluxes, footprints, block_coords, block_count, observed, obs_weight, time_cov, diffusivity
):
    time_dev, tile_rows, width = fluxes.shape
    n_space, n_tm = lax.axis_size("space"), lax.axis_size("tm")
    devices = n_space * n_tm
    obs_blocks = observed.shape[0] * n_space // LANES
    tm = lax.axis_index("tm").astype(jnp.int32).reshape(1)
    both = ("space", "tm")

    swap = [(i, i ^ 1) for i in range(n_tm)]
    parity = [list(range(n, devices, 2)) for n in range(2)]
    sums, other, kept = forward(
        tm, block_count, block_coords, fluxes, footprints, devices, obs_blocks
    )
    sums = sums + lax.ppermute(other, "tm", swap)
    sums = lax.all_to_all(sums, both, 0, 0, axis_index_groups=parity, tiled=True)
    misfit, halves = misfit_of(tm, sums, obs_weight, observed)
    halves = lax.all_to_all(halves, both, 0, 0, tiled=True)
    main, mine, other = adjoint_of(
        tm, block_count, block_coords, halves, kept, diffusivity, time_dev
    )

    def along(array, steps):
        return lax.ppermute(array, "tm", [(i, (i + 2 * steps) % n_tm) for i in range(n_tm)])

    other = lax.ppermute(other, "tm", swap)
    moves = []
    for s in range(n_space - 1):
        for t in range(0, n_tm, 2):
            moves.append((s * n_tm + t, (s + 1) * n_tm + t))
            moves.append(((s + 1) * n_tm + t + 1, s * n_tm + t + 1))
    payload, cov = lax.optimization_barrier((jnp.concatenate([other, mine], axis=0), time_cov))
    mains = [main] + [along(main, k) for k in (1, 2, 3)]
    received = lax.ppermute(payload, both, moves)
    wide = weights(tm, cov, time_dev)
    halo = received[: 2 * time_dev * SWEEPS].astype(bf16)
    last, mains[2] = lax.optimization_barrier((halo, mains[2]))
    halos = [halo, along(last, 1), along(halo, 2), along(halo, 3)]
    held = (wide, mains, halos, received, fluxes.shape)
    twin = lax.ppermute(mix(True, *held), "tm", swap)
    own = mix(False, *held)
    gradient = diffuse(tm, own, twin, diffusivity)
    return misfit.reshape(-1), gradient


def solution(mesh):
    placed = (
        P("tm", "space", None),
        P(("space", "tm"), None, None),
        P(None, ("space", "tm")),
        P(("space", "tm")),
        P("space"),
        P("space"),
        P(),
        P("space", None),
    )
    return jax.shard_map(
        body,
        mesh=mesh,
        in_specs=placed,
        out_specs=(P(("space", "tm")), P("tm", "space", None)),
        check_vma=False,
    )
```

```python
import functools

import jax
import jax.numpy as jnp
from jax import lax
from jax.experimental import pallas as pl
from jax.experimental.pallas import tpu as pltpu
from jax.sharding import PartitionSpec as P

SWEEPS = 4
LANES = 128
EDGE = 8
MIB = 1024 * 1024

f32 = jnp.float32
bf16 = jnp.bfloat16


def split2(x):
    hi = x.astype(bf16)
    return hi, (x - hi.astype(f32)).astype(bf16)


def iota(shape, dim):
    return lax.broadcasted_iota(jnp.int32, shape, dim)


def onehot(equal):
    return jnp.where(equal, 1.0, 0.0).astype(bf16)


def dot(a, b, precision=None):
    return lax.dot_general(
        a, b, (((1,), (0,)), ((), ())), preferred_element_type=f32, precision=precision
    )


def column(row):
    wide = jnp.broadcast_to(row.astype(f32), (LANES, LANES))
    return jnp.transpose(wide, (1, 0)).astype(jnp.int32)


def forward_kernel(
    tm_ref,
    count_ref,
    coords_hbm,
    flux_hbm,
    foot_ref,
    mine_ref,
    other_ref,
    keep_ref,
    coords_ref,
    flux_ref,
    rhs,
    spread,
    early,
    sems,
    small_sems,
):
    slots = foot_ref.shape[0]
    groups = slots // LANES
    time_dev, tile_rows, width = flux_ref.shape
    across = width // LANES
    steps = time_dev * tile_rows
    bounds = [0] + list(range(LANES // 2, slots, LANES)) + [slots]
    chunks = len(bounds) - 1

    def fetch(k):
        part = pl.ds(bounds[k], bounds[k + 1] - bounds[k])
        return pltpu.make_async_copy(foot_ref.at[part], keep_ref.at[part], sems.at[k])

    small = (
        pltpu.make_async_copy(coords_hbm, coords_ref, small_sems.at[0]),
        pltpu.make_async_copy(flux_hbm, flux_ref, small_sems.at[1]),
    )
    for copy in small:
        copy.start()
    fetch(0).start()
    fetch(1).start()
    for copy in small:
        copy.wait()

    flux = flux_ref[...].reshape(steps, width)
    flux = jnp.concatenate([flux[:, l * LANES : (l + 1) * LANES] for l in range(across)], axis=0)
    lane = iota((LANES, LANES), 1)
    even = (lane & 1) == 0
    for g in range(groups):
        cut = slice(g * LANES, (g + 1) * LANES)
        cell = coords_ref[1:2, cut]
        code = (cell % across) * steps + coords_ref[0:1, cut] * tile_rows + cell // across
        code = column(code)
        pick = jnp.concatenate(
            [onehot(code == lane + j * LANES) for j in range(across * steps // LANES)], axis=1
        )
        piece = jnp.transpose(dot(pick, flux), (1, 0))
        rhs[g, :LANES, :] = jnp.where(even, piece, 0.0).astype(bf16)
        rhs[g, LANES:, :] = jnp.where(even, 0.0, piece).astype(bf16)

    slot = iota((1, slots), 1)
    block = jnp.where(slot < count_ref[0], coords_ref[2:3, :], -1)
    chips, quarter, wide = mine_ref.shape
    cols = wide // LANES
    core = tm_ref[0] % 2

    def summed(n, low, high):
        row = iota((chips * quarter, high - low), 0)
        owner = row // quarter * 2 + (core if n < cols else 1 - core)
        row = (owner * quarter + row % quarter) * cols + n % cols
        full = dot(onehot(row == block[:, low:high]), spread[low:high, :])
        return full[:, :LANES] + full[:, LANES:]

    pair_of_lane = lane // 2
    batch = 8
    total = None
    for k in range(chunks):
        fetch(k).wait()
        if k + 2 < chunks:
            fetch(k + 2).start()
        for b in range(bounds[k], bounds[k + 1], 2 * batch):
            g = b // LANES
            if b % LANES == 0:
                total = jnp.zeros((LANES, LANES), f32)
            blocks = keep_ref[b : b + 2 * batch].reshape(batch, 2, LANES, LANES)
            both = jnp.concatenate([blocks[:, 0], blocks[:, 1]], axis=-1)
            result = dot(both.reshape(batch * LANES, 2 * LANES), rhs[g])
            for j in range(batch):
                p = (b % LANES) // 2 + j
                total = jnp.where(pair_of_lane == p, result[j * LANES : (j + 1) * LANES], total)
            if (b + 2 * batch) % LANES == 0:
                for n, part in enumerate(split2(jnp.transpose(total, (1, 0)))):
                    spread[g * LANES : (g + 1) * LANES, n * LANES : (n + 1) * LANES] = part
                if g == groups - 2:
                    for n in range(2 * cols):
                        early[n] = summed(n, 0, slots - LANES)
    for n in range(2 * cols):
        full = early[n] + summed(n, slots - LANES, slots)
        ref = mine_ref if n < cols else other_ref
        ref[:, :, n % cols * LANES : (n % cols + 1) * LANES] = full.reshape(chips, quarter, LANES)


def forward(tm, count, coords, fluxes, footprints, devices, obs_blocks):
    per = obs_blocks // devices
    slots = footprints.shape[0]
    cols = per // 4
    vmem = pl.BlockSpec(memory_space=pltpu.VMEM)
    smem = pl.BlockSpec(memory_space=pltpu.SMEM)
    hbm = pl.BlockSpec(memory_space=pltpu.HBM)
    return pl.pallas_call(
        forward_kernel,
        out_shape=(
            pltpu.VMEM((devices // 2, 4, cols * LANES), f32),
            pltpu.VMEM((devices // 2, 4, cols * LANES), f32),
            pltpu.VMEM(footprints.shape, bf16),
        ),
        in_specs=[smem, smem, hbm, hbm, hbm],
        out_specs=(vmem, vmem, vmem),
        scratch_shapes=[
            pltpu.VMEM(coords.shape, jnp.int32),
            pltpu.VMEM(fluxes.shape, bf16),
            pltpu.VMEM((slots // LANES, 2 * LANES, LANES), bf16),
            pltpu.VMEM((slots, 2 * LANES), bf16),
            pltpu.VMEM((2 * cols, devices * 2, LANES), f32),
            pltpu.SemaphoreType.DMA((slots // LANES + 1,)),
            pltpu.SemaphoreType.DMA((2,)),
        ],
        compiler_params=pltpu.CompilerParams(vmem_limit_bytes=38 * MIB),
        name="forward",
    )(tm, count, coords, fluxes, footprints)


def misfit_kernel(tm_ref, sums_ref, weight_ref, observed_ref, out_ref, half_ref):
    devices, quarter, wide = sums_ref.shape
    cols = wide // LANES
    total = jnp.sum(sums_ref[...], axis=0)
    base = tm_ref[0] * (quarter * cols)

    def own(ref):
        block = ref[pl.ds(base, quarter * cols), :]
        return jnp.concatenate(
            [
                jnp.concatenate(
                    [block[q * cols + l : q * cols + l + 1] for q in range(quarter)], axis=0
                )
                for l in range(cols)
            ],
            axis=1,
        )

    misfit = own(weight_ref) * (total - own(observed_ref))
    for q in range(quarter):
        for l in range(cols):
            out_ref[q * cols + l : q * cols + l + 1, :] = misfit[
                q : q + 1, l * LANES : (l + 1) * LANES
            ]
    half_ref[...] = jnp.broadcast_to(misfit[None], half_ref.shape).astype(bf16)


def misfit_of(tm, sums, weight, observed):
    devices, quarter, wide = sums.shape
    vmem = pl.BlockSpec(memory_space=pltpu.VMEM)
    return pl.pallas_call(
        misfit_kernel,
        out_shape=(
            jax.ShapeDtypeStruct((quarter * wide // LANES, LANES), f32),
            jax.ShapeDtypeStruct((2 * devices, quarter, wide), bf16),
        ),
        in_specs=[pl.BlockSpec(memory_space=pltpu.SMEM), vmem, vmem, vmem],
        out_specs=(vmem, vmem),
        compiler_params=pltpu.CompilerParams(vmem_limit_bytes=4 * MIB),
        name="misfit",
    )(tm, sums, weight.reshape(-1, LANES), observed.reshape(-1, LANES))


def adjoint_kernel(
    tm_ref,
    count_ref,
    coords_ref,
    misfit_ref,
    foot_ref,
    diff_ref,
    main_ref,
    mine_ref,
    other_ref,
    contrib,
    spread,
    rows_ref,
):
    slots = foot_ref.shape[0]
    groups = slots // LANES
    devices, quarter, wide = misfit_ref.shape
    cols = wide // LANES
    rows = devices * quarter
    tile_rows = diff_ref.shape[0]
    lane = iota((LANES, LANES), 1)
    rows_ref[...] = misfit_ref[...].astype(f32).reshape(rows, wide).astype(bf16)
    for g in range(groups):
        block = column(coords_ref[2:3, g * LANES : (g + 1) * LANES])
        chosen = jnp.zeros((LANES, LANES), f32)
        for l in range(cols):
            pick = jnp.concatenate(
                [onehot(block == (lane + j * LANES) * cols + l) for j in range(rows // LANES)], axis=1
            )
            chosen = chosen + dot(pick, rows_ref[:, l * LANES : (l + 1) * LANES])
        contrib[g * LANES : (g + 1) * LANES, :] = chosen

    batch = 16
    sub = iota((batch, LANES), 0)
    for at in range(0, slots, batch):
        some = contrib[at : at + batch, :]
        left = jnp.concatenate(
            [jnp.where(sub == j, some, 0.0).astype(bf16) for j in range(batch)], axis=1
        )
        blocks = foot_ref[at : at + batch].reshape(batch * LANES, LANES)
        for n, part in enumerate(split2(dot(left, blocks))):
            spread[at : at + batch, n * LANES : (n + 1) * LANES] = part

    time_dev = main_ref.shape[0] // tile_rows
    width = main_ref.shape[1]
    across = width // LANES
    steps = time_dev * tile_rows
    first_core = tm_ref[0] % 2 == 0
    slot = iota((1, slots), 1)
    cell = coords_ref[1:2, :]
    code = coords_ref[0:1, :] * tile_rows + cell // across
    code = jnp.where(slot < count_ref[0], code, -1)
    for l in range(across):
        cut = slice(l * LANES, (l + 1) * LANES)
        pick = onehot(iota((steps, slots), 0) == jnp.where(cell % across == l, code, -1))
        full = dot(pick, spread[...])
        summed = full[:, :LANES] + full[:, LANES:]
        main_ref[:, cut] = summed.astype(bf16)
        for t in range(time_dev):
            row, at = t * tile_rows, t * SWEEPS
            down = summed[row + tile_rows - SWEEPS : row + tile_rows]
            up = summed[row : row + SWEEPS]
            mine_ref[at : at + SWEEPS, cut] = jnp.where(first_core, down, up)
            other_ref[at : at + SWEEPS, cut] = jnp.where(first_core, up, down)
    mine_ref[time_dev * SWEEPS :, :] = jnp.where(
        first_core, diff_ref[tile_rows - EDGE :, :], diff_ref[:EDGE, :]
    )


def adjoint_of(tm, count, coords, misfit_rows, footprints, diffusivity, time_dev):
    slots = footprints.shape[0]
    tile_rows, width = diffusivity.shape
    devices, quarter, wide = misfit_rows.shape
    edge = time_dev * SWEEPS
    vmem = pl.BlockSpec(memory_space=pltpu.VMEM)
    smem = pl.BlockSpec(memory_space=pltpu.SMEM)
    return pl.pallas_call(
        adjoint_kernel,
        out_shape=(
            jax.ShapeDtypeStruct((time_dev * tile_rows, width), bf16),
            jax.ShapeDtypeStruct((edge + EDGE, width), f32),
            jax.ShapeDtypeStruct((edge, width), f32),
        ),
        in_specs=[smem, smem, vmem, vmem, vmem, vmem],
        out_specs=(vmem, vmem, vmem),
        scratch_shapes=[
            pltpu.VMEM((slots, LANES), f32),
            pltpu.VMEM((slots, 2 * LANES), bf16),
            pltpu.VMEM((devices * quarter, wide), bf16),
        ],
        compiler_params=pltpu.CompilerParams(vmem_limit_bytes=12 * MIB),
        name="adjoint",
    )(tm, count, coords, misfit_rows, footprints, diffusivity)


def spread_cov(cov, row_time, col_time, per):
    times = cov.shape[0]
    rows, cols = row_time.shape[0], col_time.shape[1]
    tall = onehot(row_time == iota((rows, times), 1)).astype(f32)
    broad = onehot(col_time == iota((times, cols), 0)).astype(f32)
    highest = lax.Precision.HIGHEST
    wide = dot(dot(tall, cov, highest), broad, highest)
    same = iota((rows, cols), 0) % per == iota((rows, cols), 1) % per
    return jnp.concatenate(split2(jnp.where(same, wide, 0.0)), axis=0)


def weights_kernel(tm_ref, cov_ref, main_ref, halo_ref):
    times = cov_ref.shape[0]
    time_dev = main_ref.shape[2] // (4 * EDGE)
    depth, core = tm_ref[0] // 2, tm_ref[0] % 2

    def target_time(per, n):
        row = iota((time_dev * per, times), 0)
        return (2 * depth + (core if n == 0 else 1 - core)) * time_dev + row // per

    def depth_of(col, block):
        return (depth + 4 - col // block) % 4

    block = EDGE * time_dev
    col = iota((times, 4 * block), 1)
    source = (2 * depth_of(col, block) + core) * time_dev + col % block // EDGE
    half = SWEEPS * time_dev
    col = iota((times, 8 * half), 1)
    core_of = jnp.where(col % (2 * half) < half, 1 - core, core)
    edge_source = (2 * depth_of(col, 2 * half) + core_of) * time_dev + col % half // SWEEPS
    for n in range(2):
        main_ref[n] = spread_cov(cov_ref[...], target_time(EDGE, n), source, EDGE)
        halo_ref[n] = spread_cov(cov_ref[...], target_time(SWEEPS, n), edge_source, SWEEPS)


def weights(tm, cov, time_dev):
    vmem = pl.BlockSpec(memory_space=pltpu.VMEM)
    block = time_dev * EDGE
    half = time_dev * SWEEPS
    return pl.pallas_call(
        weights_kernel,
        out_shape=(
            jax.ShapeDtypeStruct((2, 2 * block, 4 * block), bf16),
            jax.ShapeDtypeStruct((2, 2 * half, 8 * half), bf16),
        ),
        in_specs=[pl.BlockSpec(memory_space=pltpu.SMEM), vmem],
        out_specs=(vmem, vmem),
        compiler_params=pltpu.CompilerParams(vmem_limit_bytes=2 * MIB),
        name="weights",
    )(tm, cov)


def mix_kernel(twin, main_weight_ref, halo_weight_ref, *refs):
    mains, halos, received_ref, out_ref = refs[:4], refs[4:8], refs[8], refs[9]
    time_dev, ext_rows, width = out_ref.shape
    tile_rows = ext_rows - EDGE

    def put(full, at, count):
        half = full.shape[0] // 2
        full = full[:half] + full[half:]
        for t in range(time_dev):
            out_ref[t, at : at + count, :] = full[t * count : (t + 1) * count]

    wide = main_weight_ref[int(twin)]
    for r in range(0, tile_rows, EDGE):
        pieces = [
            main[u * tile_rows + r : u * tile_rows + r + EDGE, :].astype(f32)
            for main in mains
            for u in range(time_dev)
        ]
        put(dot(wide, jnp.concatenate(pieces, axis=0).astype(bf16)), r, EDGE)
    edges = jnp.concatenate([halo[...] for halo in halos], axis=0)
    put(dot(halo_weight_ref[int(twin)], edges), tile_rows, SWEEPS)
    base = 2 * time_dev * SWEEPS
    for t in range(time_dev):
        n = base + (t % 2) * SWEEPS
        out_ref[t, tile_rows + SWEEPS :, :] = received_ref[n : n + SWEEPS, :]


def mix(twin, wide, mains, halos, received, shape):
    vmem = pl.BlockSpec(memory_space=pltpu.VMEM)
    return pl.pallas_call(
        functools.partial(mix_kernel, twin),
        out_shape=jax.ShapeDtypeStruct((shape[0], shape[1] + EDGE, shape[2]), f32),
        in_specs=[vmem] * 11,
        out_specs=vmem,
        compiler_params=pltpu.CompilerParams(vmem_limit_bytes=8 * MIB),
        name="mix_twin" if twin else "mix_own",
    )(*wide, *mains, *halos, received)


def diffuse_kernel(tm_ref, own_ref, twin_ref, diff_ref, out_ref, field, other, staged, sems):
    time_dev, tile_rows, width = staged.shape
    ext_rows = field.shape[1]
    first, last = 2 * EDGE, 2 * EDGE + tile_rows
    first_core = tm_ref[0] % 2 == 0
    lower = tile_rows + SWEEPS

    def halo_of(ref):
        return jnp.concatenate([ref[0, lower:, :], ref[1, lower:, :]], axis=0)

    def ordered(a, b):
        return jnp.where(first_core, a, b), jnp.where(first_core, b, a)

    def leave(t):
        return pltpu.make_async_copy(staged.at[t], out_ref.at[t], sems.at[t])

    before, after = ordered(halo_of(own_ref), halo_of(twin_ref))
    diff = jnp.concatenate([before, diff_ref[...], after], axis=0)
    keep = 1.0 - 4.0 * diff
    column_of = iota(diff.shape, 1)
    here = slice(EDGE, ext_rows - EDGE)
    for buffer in (field, other):
        for t in range(time_dev):
            buffer[t, :first, :] = jnp.zeros((first, width), f32)
            buffer[t, last:, :] = jnp.zeros((ext_rows - last, width), f32)
    for t in range(time_dev):
        field[t, first:last, :] = own_ref[t, :tile_rows, :] + twin_ref[t, :tile_rows, :]
        above, below = ordered(own_ref[t, tile_rows:lower, :], twin_ref[t, tile_rows:lower, :])
        field[t, first - SWEEPS : first, :] = above
        field[t, last : last + SWEEPS, :] = below
    source, target = field, other
    for sweep in range(SWEEPS):
        for t in range(time_dev):
            centre = source[t, here, :]
            left = jnp.where(column_of == 0, 0.0, pltpu.roll(centre, 1, 1))
            right = jnp.where(column_of == width - 1, 0.0, pltpu.roll(centre, width - 1, 1))
            above = source[t, EDGE - 1 : ext_rows - EDGE - 1, :]
            below = source[t, EDGE + 1 : ext_rows - EDGE + 1, :]
            moved = keep * centre + diff * (below + above + right + left)
            if sweep + 1 < SWEEPS:
                target[t, here, :] = moved
            else:
                staged[t] = moved[EDGE : EDGE + tile_rows]
                leave(t).start()
        source, target = target, source
    for t in range(time_dev):
        leave(t).wait()


def diffuse(tm, own, twin, diffusivity):
    time_dev = own.shape[0]
    tile_rows, width = diffusivity.shape
    field = pltpu.VMEM((time_dev, tile_rows + 4 * EDGE, width), f32)
    vmem = pl.BlockSpec(memory_space=pltpu.VMEM)
    shape = (time_dev, tile_rows, width)
    return pl.pallas_call(
        diffuse_kernel,
        out_shape=jax.ShapeDtypeStruct(shape, f32),
        in_specs=[pl.BlockSpec(memory_space=pltpu.SMEM)] + [vmem] * 3,
        out_specs=pl.BlockSpec(memory_space=pltpu.HBM),
        scratch_shapes=[field, field, pltpu.VMEM(shape, f32), pltpu.SemaphoreType.DMA((time_dev,))],
        compiler_params=pltpu.CompilerParams(vmem_limit_bytes=10 * MIB),
        name="diffuse",
    )(tm, own, twin, diffusivity)


def body(
    fluxes, footprints, block_coords, block_count, observed, obs_weight, time_cov, diffusivity
):
    time_dev, tile_rows, width = fluxes.shape
    n_space, n_tm = lax.axis_size("space"), lax.axis_size("tm")
    devices = n_space * n_tm
    obs_blocks = observed.shape[0] * n_space // LANES
    tm = lax.axis_index("tm").astype(jnp.int32).reshape(1)
    both = ("space", "tm")

    swap = [(i, i ^ 1) for i in range(n_tm)]
    parity = [list(range(n, devices, 2)) for n in range(2)]
    sums, other, kept = forward(
        tm, block_count, block_coords, fluxes, footprints, devices, obs_blocks
    )
    sums = sums + lax.ppermute(other, "tm", swap)
    sums = lax.all_to_all(sums, both, 0, 0, axis_index_groups=parity, tiled=True)
    misfit, halves = misfit_of(tm, sums, obs_weight, observed)
    halves = lax.all_to_all(halves, both, 0, 0, tiled=True)
    main, mine, other = adjoint_of(
        tm, block_count, block_coords, halves, kept, diffusivity, time_dev
    )

    def along(array, steps):
        return lax.ppermute(array, "tm", [(i, (i + 2 * steps) % n_tm) for i in range(n_tm)])

    other = lax.ppermute(other, "tm", swap)
    moves = []
    for s in range(n_space - 1):
        for t in range(0, n_tm, 2):
            moves.append((s * n_tm + t, (s + 1) * n_tm + t))
            moves.append(((s + 1) * n_tm + t + 1, s * n_tm + t + 1))
    payload, cov = lax.optimization_barrier((jnp.concatenate([other, mine], axis=0), time_cov))
    mains = [main] + [along(main, k) for k in (1, 2, 3)]
    received = lax.ppermute(payload, both, moves)
    wide = weights(tm, cov, time_dev)
    halo = received[: 2 * time_dev * SWEEPS].astype(bf16)
    last, mains[2] = lax.optimization_barrier((halo, mains[2]))
    halos = [halo, along(halo, 1), along(halo, 2), along(last, 3)]
    held = (wide, mains, halos, received, fluxes.shape)
    twin = lax.ppermute(mix(True, *held), "tm", swap)
    own = mix(False, *held)
    gradient = diffuse(tm, own, twin, diffusivity)
    return misfit.reshape(-1), gradient


def solution(mesh):
    placed = (
        P("tm", "space", None),
        P(("space", "tm"), None, None),
        P(None, ("space", "tm")),
        P(("space", "tm")),
        P("space"),
        P("space"),
        P(),
        P("space", None),
    )
    return jax.shard_map(
        body,
        mesh=mesh,
        in_specs=placed,
        out_specs=(P(("space", "tm")), P("tm", "space", None)),
        check_vma=False,
    )
```

```python
import functools

import jax
import jax.numpy as jnp
from jax import lax
from jax.experimental import pallas as pl
from jax.experimental.pallas import tpu as pltpu
from jax.sharding import PartitionSpec as P

SWEEPS = 4
LANES = 128
EDGE = 8
MIB = 1024 * 1024

f32 = jnp.float32
bf16 = jnp.bfloat16


def split2(x):
    hi = x.astype(bf16)
    return hi, (x - hi.astype(f32)).astype(bf16)


def iota(shape, dim):
    return lax.broadcasted_iota(jnp.int32, shape, dim)


def onehot(equal):
    return jnp.where(equal, 1.0, 0.0).astype(bf16)


def dot(a, b, precision=None):
    return lax.dot_general(
        a, b, (((1,), (0,)), ((), ())), preferred_element_type=f32, precision=precision
    )


def column(row):
    wide = jnp.broadcast_to(row.astype(f32), (LANES, LANES))
    return jnp.transpose(wide, (1, 0)).astype(jnp.int32)


def forward_kernel(
    tm_ref,
    count_ref,
    coords_hbm,
    flux_hbm,
    foot_ref,
    mine_ref,
    other_ref,
    keep_ref,
    coords_ref,
    flux_ref,
    rhs,
    spread,
    early,
    sems,
    small_sems,
):
    slots = foot_ref.shape[0]
    groups = slots // LANES
    time_dev, tile_rows, width = flux_ref.shape
    across = width // LANES
    steps = time_dev * tile_rows
    bounds = [0] + list(range(LANES // 2, slots, LANES)) + [slots]
    chunks = len(bounds) - 1

    def fetch(k):
        part = pl.ds(bounds[k], bounds[k + 1] - bounds[k])
        return pltpu.make_async_copy(foot_ref.at[part], keep_ref.at[part], sems.at[k])

    small = (
        pltpu.make_async_copy(coords_hbm, coords_ref, small_sems.at[0]),
        pltpu.make_async_copy(flux_hbm, flux_ref, small_sems.at[1]),
    )
    for copy in small:
        copy.start()
    fetch(0).start()
    fetch(1).start()
    for copy in small:
        copy.wait()

    flux = flux_ref[...].reshape(steps, width)
    flux = jnp.concatenate([flux[:, l * LANES : (l + 1) * LANES] for l in range(across)], axis=0)
    lane = iota((LANES, LANES), 1)
    even = (lane & 1) == 0
    for g in range(groups):
        cut = slice(g * LANES, (g + 1) * LANES)
        cell = coords_ref[1:2, cut]
        code = (cell % across) * steps + coords_ref[0:1, cut] * tile_rows + cell // across
        code = column(code)
        pick = jnp.concatenate(
            [onehot(code == lane + j * LANES) for j in range(across * steps // LANES)], axis=1
        )
        piece = jnp.transpose(dot(pick, flux), (1, 0))
        rhs[g, :LANES, :] = jnp.where(even, piece, 0.0).astype(bf16)
        rhs[g, LANES:, :] = jnp.where(even, 0.0, piece).astype(bf16)

    slot = iota((1, slots), 1)
    block = jnp.where(slot < count_ref[0], coords_ref[2:3, :], -1)
    chips, quarter, wide = mine_ref.shape
    cols = wide // LANES
    core = tm_ref[0] % 2

    def summed(n, low, high):
        row = iota((chips * quarter, high - low), 0)
        owner = row // quarter * 2 + (core if n < cols else 1 - core)
        row = (owner * quarter + row % quarter) * cols + n % cols
        full = dot(onehot(row == block[:, low:high]), spread[low:high, :])
        return full[:, :LANES] + full[:, LANES:]

    pair_of_lane = lane // 2
    batch = 8
    total = None
    for k in range(chunks):
        fetch(k).wait()
        if k + 2 < chunks:
            fetch(k + 2).start()
        for b in range(bounds[k], bounds[k + 1], 2 * batch):
            g = b // LANES
            if b % LANES == 0:
                total = jnp.zeros((LANES, LANES), f32)
            blocks = keep_ref[b : b + 2 * batch].reshape(batch, 2, LANES, LANES)
            both = jnp.concatenate([blocks[:, 0], blocks[:, 1]], axis=-1)
            result = dot(both.reshape(batch * LANES, 2 * LANES), rhs[g])
            for j in range(batch):
                p = (b % LANES) // 2 + j
                total = jnp.where(pair_of_lane == p, result[j * LANES : (j + 1) * LANES], total)
            if (b + 2 * batch) % LANES == 0:
                for n, part in enumerate(split2(jnp.transpose(total, (1, 0)))):
                    spread[g * LANES : (g + 1) * LANES, n * LANES : (n + 1) * LANES] = part
                if g == groups - 2:
                    for n in range(2 * cols):
                        early[n] = summed(n, 0, slots - LANES)
    for n in range(2 * cols):
        full = early[n] + summed(n, slots - LANES, slots)
        ref = mine_ref if n < cols else other_ref
        ref[:, :, n % cols * LANES : (n % cols + 1) * LANES] = full.reshape(chips, quarter, LANES)


def forward(tm, count, coords, fluxes, footprints, devices, obs_blocks):
    per = obs_blocks // devices
    slots = footprints.shape[0]
    cols = per // 4
    vmem = pl.BlockSpec(memory_space=pltpu.VMEM)
    smem = pl.BlockSpec(memory_space=pltpu.SMEM)
    hbm = pl.BlockSpec(memory_space=pltpu.HBM)
    return pl.pallas_call(
        forward_kernel,
        out_shape=(
            pltpu.VMEM((devices // 2, 4, cols * LANES), f32),
            pltpu.VMEM((devices // 2, 4, cols * LANES), f32),
            pltpu.VMEM(footprints.shape, bf16),
        ),
        in_specs=[smem, smem, hbm, hbm, hbm],
        out_specs=(vmem, vmem, vmem),
        scratch_shapes=[
            pltpu.VMEM(coords.shape, jnp.int32),
            pltpu.VMEM(fluxes.shape, bf16),
            pltpu.VMEM((slots // LANES, 2 * LANES, LANES), bf16),
            pltpu.VMEM((slots, 2 * LANES), bf16),
            pltpu.VMEM((2 * cols, devices * 2, LANES), f32),
            pltpu.SemaphoreType.DMA((slots // LANES + 1,)),
            pltpu.SemaphoreType.DMA((2,)),
        ],
        compiler_params=pltpu.CompilerParams(vmem_limit_bytes=38 * MIB),
        name="forward",
    )(tm, count, coords, fluxes, footprints)


def misfit_kernel(tm_ref, sums_ref, weight_ref, observed_ref, out_ref, half_ref):
    devices, quarter, wide = sums_ref.shape
    cols = wide // LANES
    total = jnp.sum(sums_ref[...], axis=0)
    base = tm_ref[0] * (quarter * cols)

    def own(ref):
        block = ref[pl.ds(base, quarter * cols), :]
        return jnp.concatenate(
            [
                jnp.concatenate(
                    [block[q * cols + l : q * cols + l + 1] for q in range(quarter)], axis=0
                )
                for l in range(cols)
            ],
            axis=1,
        )

    misfit = own(weight_ref) * (total - own(observed_ref))
    for q in range(quarter):
        for l in range(cols):
            out_ref[q * cols + l : q * cols + l + 1, :] = misfit[
                q : q + 1, l * LANES : (l + 1) * LANES
            ]
    half_ref[...] = jnp.broadcast_to(misfit[None], half_ref.shape).astype(bf16)


def misfit_of(tm, sums, weight, observed):
    devices, quarter, wide = sums.shape
    vmem = pl.BlockSpec(memory_space=pltpu.VMEM)
    return pl.pallas_call(
        misfit_kernel,
        out_shape=(
            jax.ShapeDtypeStruct((quarter * wide // LANES, LANES), f32),
            jax.ShapeDtypeStruct((2 * devices, quarter, wide), bf16),
        ),
        in_specs=[pl.BlockSpec(memory_space=pltpu.SMEM), vmem, vmem, vmem],
        out_specs=(vmem, vmem),
        compiler_params=pltpu.CompilerParams(vmem_limit_bytes=4 * MIB),
        name="misfit",
    )(tm, sums, weight.reshape(-1, LANES), observed.reshape(-1, LANES))


def adjoint_kernel(
    tm_ref,
    count_ref,
    coords_ref,
    misfit_ref,
    foot_ref,
    diff_ref,
    main_ref,
    mine_ref,
    other_ref,
    contrib,
    spread,
    rows_ref,
):
    slots = foot_ref.shape[0]
    groups = slots // LANES
    devices, quarter, wide = misfit_ref.shape
    cols = wide // LANES
    rows = devices * quarter
    tile_rows = diff_ref.shape[0]
    lane = iota((LANES, LANES), 1)
    rows_ref[...] = misfit_ref[...].astype(f32).reshape(rows, wide).astype(bf16)
    for g in range(groups):
        block = column(coords_ref[2:3, g * LANES : (g + 1) * LANES])
        chosen = jnp.zeros((LANES, LANES), f32)
        for l in range(cols):
            pick = jnp.concatenate(
                [onehot(block == (lane + j * LANES) * cols + l) for j in range(rows // LANES)], axis=1
            )
            chosen = chosen + dot(pick, rows_ref[:, l * LANES : (l + 1) * LANES])
        contrib[g * LANES : (g + 1) * LANES, :] = chosen

    batch = 16
    sub = iota((batch, LANES), 0)
    for at in range(0, slots, batch):
        some = contrib[at : at + batch, :]
        left = jnp.concatenate(
            [jnp.where(sub == j, some, 0.0).astype(bf16) for j in range(batch)], axis=1
        )
        blocks = foot_ref[at : at + batch].reshape(batch * LANES, LANES)
        for n, part in enumerate(split2(dot(left, blocks))):
            spread[at : at + batch, n * LANES : (n + 1) * LANES] = part

    time_dev = main_ref.shape[0] // tile_rows
    width = main_ref.shape[1]
    across = width // LANES
    steps = time_dev * tile_rows
    first_core = tm_ref[0] % 2 == 0
    slot = iota((1, slots), 1)
    cell = coords_ref[1:2, :]
    code = coords_ref[0:1, :] * tile_rows + cell // across
    code = jnp.where(slot < count_ref[0], code, -1)
    for l in range(across):
        cut = slice(l * LANES, (l + 1) * LANES)
        pick = onehot(iota((steps, slots), 0) == jnp.where(cell % across == l, code, -1))
        full = dot(pick, spread[...])
        summed = full[:, :LANES] + full[:, LANES:]
        main_ref[:, cut] = summed.astype(bf16)
        up, down = (
            jnp.concatenate(
                [summed[n * tile_rows + at : n * tile_rows + at + SWEEPS] for n in range(time_dev)],
                axis=0,
            )
            for at in (0, tile_rows - SWEEPS)
        )
        mine_ref[: time_dev * SWEEPS, cut] = jnp.where(first_core, down, up).astype(bf16)
        other_ref[:, cut] = jnp.where(first_core, up, down).astype(bf16)
    edge = jnp.where(first_core, diff_ref[tile_rows - EDGE :, :], diff_ref[:EDGE, :])
    high, rest = split2(edge)
    low = edge - high.astype(f32) - rest.astype(f32)
    parts = jnp.concatenate(
        [high.astype(f32), rest.astype(f32), low, jnp.zeros_like(low)], axis=0
    )
    mine_ref[time_dev * SWEEPS :, :] = parts.astype(bf16)


def adjoint_of(tm, count, coords, misfit_rows, footprints, diffusivity, time_dev):
    slots = footprints.shape[0]
    tile_rows, width = diffusivity.shape
    devices, quarter, wide = misfit_rows.shape
    edge = time_dev * SWEEPS
    vmem = pl.BlockSpec(memory_space=pltpu.VMEM)
    smem = pl.BlockSpec(memory_space=pltpu.SMEM)
    return pl.pallas_call(
        adjoint_kernel,
        out_shape=(
            jax.ShapeDtypeStruct((time_dev * tile_rows, width), bf16),
            jax.ShapeDtypeStruct((edge + 4 * EDGE, width), bf16),
            jax.ShapeDtypeStruct((edge, width), bf16),
        ),
        in_specs=[smem, smem, vmem, vmem, vmem, vmem],
        out_specs=(vmem, vmem, vmem),
        scratch_shapes=[
            pltpu.VMEM((slots, LANES), f32),
            pltpu.VMEM((slots, 2 * LANES), bf16),
            pltpu.VMEM((devices * quarter, wide), bf16),
        ],
        compiler_params=pltpu.CompilerParams(vmem_limit_bytes=12 * MIB),
        name="adjoint",
    )(tm, count, coords, misfit_rows, footprints, diffusivity)


def spread_cov(cov, row_time, col_time, per):
    times = cov.shape[0]
    rows, cols = row_time.shape[0], col_time.shape[1]
    tall = onehot(row_time == iota((rows, times), 1)).astype(f32)
    broad = onehot(col_time == iota((times, cols), 0)).astype(f32)
    highest = lax.Precision.HIGHEST
    wide = dot(dot(tall, cov, highest), broad, highest)
    same = iota((rows, cols), 0) % per == iota((rows, cols), 1) % per
    return jnp.concatenate(split2(jnp.where(same, wide, 0.0)), axis=0)


def weights_kernel(tm_ref, cov_ref, main_ref, halo_ref):
    times = cov_ref.shape[0]
    time_dev = main_ref.shape[2] // (4 * EDGE)
    depth, core = tm_ref[0] // 2, tm_ref[0] % 2

    def target_time(per, n):
        row = iota((time_dev * per, times), 0)
        return (2 * depth + (core if n == 0 else 1 - core)) * time_dev + row // per

    def depth_of(col, block):
        return (depth + 4 - col // block) % 4

    block = EDGE * time_dev
    col = iota((times, 4 * block), 1)
    source = (2 * depth_of(col, block) + core) * time_dev + col % block // EDGE
    half = SWEEPS * time_dev
    col = iota((times, 8 * half), 1)
    core_of = jnp.where(col % (2 * half) < half, 1 - core, core)
    edge_source = (2 * depth_of(col, 2 * half) + core_of) * time_dev + col % half // SWEEPS
    for n in range(2):
        main_ref[n] = spread_cov(cov_ref[...], target_time(EDGE, n), source, EDGE)
        halo_ref[n] = spread_cov(cov_ref[...], target_time(SWEEPS, n), edge_source, SWEEPS)


def weights(tm, cov, time_dev):
    vmem = pl.BlockSpec(memory_space=pltpu.VMEM)
    block = time_dev * EDGE
    half = time_dev * SWEEPS
    return pl.pallas_call(
        weights_kernel,
        out_shape=(
            jax.ShapeDtypeStruct((2, 2 * block, 4 * block), bf16),
            jax.ShapeDtypeStruct((2, 2 * half, 8 * half), bf16),
        ),
        in_specs=[pl.BlockSpec(memory_space=pltpu.SMEM), vmem],
        out_specs=(vmem, vmem),
        compiler_params=pltpu.CompilerParams(vmem_limit_bytes=2 * MIB),
        name="weights",
    )(tm, cov)


def mix_kernel(twin, main_weight_ref, halo_weight_ref, *refs):
    mains, halos, received_ref, out_ref = refs[:4], refs[4:8], refs[8], refs[9]
    time_dev, ext_rows, width = out_ref.shape
    tile_rows = ext_rows - EDGE

    def put(full, at, count):
        half = full.shape[0] // 2
        full = full[:half] + full[half:]
        for t in range(time_dev):
            out_ref[t, at : at + count, :] = full[t * count : (t + 1) * count]

    wide = main_weight_ref[int(twin)]
    for r in range(0, tile_rows, EDGE):
        pieces = [
            main[u * tile_rows + r : u * tile_rows + r + EDGE, :].astype(f32)
            for main in mains
            for u in range(time_dev)
        ]
        put(dot(wide, jnp.concatenate(pieces, axis=0).astype(bf16)), r, EDGE)
    edges = jnp.concatenate([halo[...] for halo in halos], axis=0)
    put(dot(halo_weight_ref[int(twin)], edges), tile_rows, SWEEPS)
    parts = received_ref[2 * time_dev * SWEEPS :, :].astype(f32)
    diff = parts[:EDGE] + parts[EDGE : 2 * EDGE] + parts[2 * EDGE : 3 * EDGE]
    for t in range(time_dev):
        n = (t % 2) * SWEEPS
        out_ref[t, tile_rows + SWEEPS :, :] = diff[n : n + SWEEPS]


def mix(twin, wide, mains, halos, received, shape):
    vmem = pl.BlockSpec(memory_space=pltpu.VMEM)
    return pl.pallas_call(
        functools.partial(mix_kernel, twin),
        out_shape=jax.ShapeDtypeStruct((shape[0], shape[1] + EDGE, shape[2]), f32),
        in_specs=[vmem] * 11,
        out_specs=vmem,
        compiler_params=pltpu.CompilerParams(vmem_limit_bytes=8 * MIB),
        name="mix_twin" if twin else "mix_own",
    )(*wide, *mains, *halos, received)


def diffuse_kernel(tm_ref, own_ref, twin_ref, diff_ref, out_ref, field, other, staged, sems):
    time_dev, tile_rows, width = staged.shape
    ext_rows = field.shape[1]
    first, last = 2 * EDGE, 2 * EDGE + tile_rows
    first_core = tm_ref[0] % 2 == 0
    lower = tile_rows + SWEEPS

    def halo_of(ref):
        return jnp.concatenate([ref[0, lower:, :], ref[1, lower:, :]], axis=0)

    def ordered(a, b):
        return jnp.where(first_core, a, b), jnp.where(first_core, b, a)

    def leave(t):
        return pltpu.make_async_copy(staged.at[t], out_ref.at[t], sems.at[t])

    before, after = ordered(halo_of(own_ref), halo_of(twin_ref))
    diff = jnp.concatenate([before, diff_ref[...], after], axis=0)
    keep = 1.0 - 4.0 * diff
    column_of = iota(diff.shape, 1)
    here = slice(EDGE, ext_rows - EDGE)
    for buffer in (field, other):
        for t in range(time_dev):
            buffer[t, :first, :] = jnp.zeros((first, width), f32)
            buffer[t, last:, :] = jnp.zeros((ext_rows - last, width), f32)
    for t in range(time_dev):
        field[t, first:last, :] = own_ref[t, :tile_rows, :] + twin_ref[t, :tile_rows, :]
        above, below = ordered(own_ref[t, tile_rows:lower, :], twin_ref[t, tile_rows:lower, :])
        field[t, first - SWEEPS : first, :] = above
        field[t, last : last + SWEEPS, :] = below
    source, target = field, other
    for sweep in range(SWEEPS):
        for t in range(time_dev):
            centre = source[t, here, :]
            left = jnp.where(column_of == 0, 0.0, pltpu.roll(centre, 1, 1))
            right = jnp.where(column_of == width - 1, 0.0, pltpu.roll(centre, width - 1, 1))
            above = source[t, EDGE - 1 : ext_rows - EDGE - 1, :]
            below = source[t, EDGE + 1 : ext_rows - EDGE + 1, :]
            moved = keep * centre + diff * (below + above + right + left)
            if sweep + 1 < SWEEPS:
                target[t, here, :] = moved
            else:
                staged[t] = moved[EDGE : EDGE + tile_rows]
                leave(t).start()
        source, target = target, source
    for t in range(time_dev):
        leave(t).wait()


def diffuse(tm, own, twin, diffusivity):
    time_dev = own.shape[0]
    tile_rows, width = diffusivity.shape
    field = pltpu.VMEM((time_dev, tile_rows + 4 * EDGE, width), f32)
    vmem = pl.BlockSpec(memory_space=pltpu.VMEM)
    shape = (time_dev, tile_rows, width)
    return pl.pallas_call(
        diffuse_kernel,
        out_shape=jax.ShapeDtypeStruct(shape, f32),
        in_specs=[pl.BlockSpec(memory_space=pltpu.SMEM)] + [vmem] * 3,
        out_specs=pl.BlockSpec(memory_space=pltpu.HBM),
        scratch_shapes=[field, field, pltpu.VMEM(shape, f32), pltpu.SemaphoreType.DMA((time_dev,))],
        compiler_params=pltpu.CompilerParams(vmem_limit_bytes=10 * MIB),
        name="diffuse",
    )(tm, own, twin, diffusivity)


def body(
    fluxes, footprints, block_coords, block_count, observed, obs_weight, time_cov, diffusivity
):
    time_dev, tile_rows, width = fluxes.shape
    n_space, n_tm = lax.axis_size("space"), lax.axis_size("tm")
    devices = n_space * n_tm
    obs_blocks = observed.shape[0] * n_space // LANES
    tm = lax.axis_index("tm").astype(jnp.int32).reshape(1)
    both = ("space", "tm")

    swap = [(i, i ^ 1) for i in range(n_tm)]
    parity = [list(range(n, devices, 2)) for n in range(2)]
    sums, other, kept = forward(
        tm, block_count, block_coords, fluxes, footprints, devices, obs_blocks
    )
    sums = sums + lax.ppermute(other, "tm", swap)
    sums = lax.all_to_all(sums, both, 0, 0, axis_index_groups=parity, tiled=True)
    misfit, halves = misfit_of(tm, sums, obs_weight, observed)
    halves = lax.all_to_all(halves, both, 0, 0, tiled=True)
    main, mine, other = adjoint_of(
        tm, block_count, block_coords, halves, kept, diffusivity, time_dev
    )

    def along(array, steps):
        return lax.ppermute(array, "tm", [(i, (i + 2 * steps) % n_tm) for i in range(n_tm)])

    other = lax.ppermute(other, "tm", swap)
    moves = []
    for s in range(n_space - 1):
        for t in range(0, n_tm, 2):
            moves.append((s * n_tm + t, (s + 1) * n_tm + t))
            moves.append(((s + 1) * n_tm + t + 1, s * n_tm + t + 1))
    payload, cov = lax.optimization_barrier((jnp.concatenate([other, mine], axis=0), time_cov))
    mains = [main] + [along(main, k) for k in (1, 2, 3)]
    received = lax.ppermute(payload, both, moves)
    wide = weights(tm, cov, time_dev)
    halo = received[: 2 * time_dev * SWEEPS]
    last, mains[2] = lax.optimization_barrier((halo, mains[2]))
    halos = [halo, along(halo, 1), along(halo, 2), along(last, 3)]
    held = (wide, mains, halos, received, fluxes.shape)
    twin = lax.ppermute(mix(True, *held), "tm", swap)
    own = mix(False, *held)
    gradient = diffuse(tm, own, twin, diffusivity)
    return misfit.reshape(-1), gradient


def solution(mesh):
    placed = (
        P("tm", "space", None),
        P(("space", "tm"), None, None),
        P(None, ("space", "tm")),
        P(("space", "tm")),
        P("space"),
        P("space"),
        P(),
        P("space", None),
    )
    return jax.shard_map(
        body,
        mesh=mesh,
        in_specs=placed,
        out_specs=(P(("space", "tm")), P("tm", "space", None)),
        check_vma=False,
    )
```
